32 devices in a mesh: grp: 2 (over x), col: 16 (over z, y, core).
Axes of the slice: x: 2, y: 2, z: 4, core: 2. Of those that a mesh axis runs over, the one named last changes fastest.
Arguments:
- database: int32 [256, 4096], P('col', 'grp'), parts along dimension 1, may hold values from 0 to 255
- queries: int32 [16, 256], P('grp', 'col'), parts along dimension 0, may hold values from -2147483648 to 2147483646
- key_rows: int32 [16, 8192], P('grp', 'col'), parts along dimension 0, may hold values from -2147483648 to 2147483646
- hint: int32 [4, 1024], P('grp'), parts along dimension 0, may hold values from -2147483648 to 2147483646
- assignment: int32 [32], P('grp'), parts along dimension 0, may hold values from 0 to 15, each once
Outputs:
- packed: float32 [32, 2, 1024], P(('grp', 'col')), parts along dimension 0
The draws below stay inside these ranges and needn't reach their ends.
There are 2 independent parts, one for each index of `grp`. The reference program is written for one: setup_inputs(seed, part) draws one part's arguments, and reference() takes and returns one part's arrays. A program takes and returns all parts, laid end to end along the dimension named above; each array names one. Nothing has to cross between parts.
Inputs may be any that keep to these rules, and one draw needn't show every extreme that they name: `assignment`: every unit appears in exactly one slot.
All inputs are finite; a program needn't handle non-finite values.
Results may differ from the reference program's by a relative error of at most 0.0003.
Values sent between devices are 32-bit elements; how exact they have to be, the bound alone decides.
No kernel may reach another device: no remote copies, remote signals or barrier semaphores. Data moves between devices by JAX's collectives and lax.ppermute only.
A program may use at most 128 MiB of HBM per device.

```python
import jax
import jax.numpy as jnp
from jax import lax

CYCLE = 1024
LEVELS = 2
DIGITS = 2
CLIENTS = 8
POLYS = 2
ROWS = 2048
COLS = 256
UNITS = 16
KEY_LEN = 8192


def plant(result, key, least, top_value):
    longest = result.shape.index(max(result.shape))
    spots = []
    for shift in (0, 1):
        where = [jax.random.randint(jax.random.fold_in(key, axis), (), 0, length) for axis, length in enumerate(result.shape)]
        where[longest] = (where[longest] + shift) % result.shape[longest]
        spots.append(tuple(where))
    return result.at[spots[0]].set(least).at[spots[1]].set(top_value)


def setup_inputs(seed: int = 0, part: int = 0) -> dict:
    seeds = jax.random.split(jax.random.key(seed), 6)
    part_keys = jax.random.split(jax.random.fold_in(seeds[5], part), 6)
    database = plant(jax.random.randint(part_keys[0], (COLS, ROWS), 0, 256), jax.random.fold_in(part_keys[0], 1), 0, 255).astype(jnp.int32)
    queries = plant(jax.random.randint(part_keys[1], (CLIENTS, COLS), -2147483648, 2147483647), jax.random.fold_in(part_keys[1], 1), -2147483648, 2147483646).astype(jnp.int32)
    key_rows = plant(jax.random.randint(part_keys[2], (CLIENTS, KEY_LEN), -2147483648, 2147483647), jax.random.fold_in(part_keys[2], 1), -2147483648, 2147483646).astype(jnp.int32)
    hint = plant(jax.random.randint(part_keys[3], (POLYS, CYCLE), -2147483648, 2147483647), jax.random.fold_in(part_keys[3], 1), -2147483648, 2147483646).astype(jnp.int32)
    assignment = jax.random.permutation(part_keys[4], UNITS).astype(jnp.int32)
    return {"database": database, "queries": queries, "key_rows": key_rows, "hint": hint, "assignment": assignment}


def automorph(polynomial, galois):
    cycle_width = polynomial.shape[0]
    inverse = pow(galois, -1, 2 * cycle_width)
    source = (jnp.arange(cycle_width, dtype=jnp.int32) * inverse) % (2 * cycle_width)
    picked = jnp.take(polynomial, source % cycle_width, axis=0)
    return jnp.where(source < cycle_width, picked, -picked)


def toeplitz(key_poly):
    cycle_width = key_poly.shape[0]
    shifted = jnp.concatenate([-key_poly[1:], key_poly, -key_poly[:1]])
    tiled_rows = jnp.tile(shifted, cycle_width)[: cycle_width * (2 * cycle_width - 1)]
    return tiled_rows.reshape(cycle_width, 2 * cycle_width - 1)[:, cycle_width - 1:2 * cycle_width - 1]


def switch_section(mask_poly, value_poly, section_keys, galois):
    cycle_width = mask_poly.shape[0]
    rotated_mask = automorph(mask_poly, galois)
    rotated_value = automorph(value_poly, galois)
    switched = jnp.zeros((2 * cycle_width,), jnp.int32)
    for digit_index in range(section_keys.shape[0]):
        digit_row = jnp.bitwise_and(jnp.right_shift(rotated_mask, 16 * digit_index), 65535)
        matrix = jnp.concatenate([toeplitz(section_keys[digit_index, 0]), toeplitz(section_keys[digit_index, 1])], axis=1)
        switched = switched + jnp.dot(digit_row[None, :], matrix, preferred_element_type=jnp.int32)[0]
    return mask_poly + switched[:cycle_width], value_poly + rotated_value + switched[cycle_width:]


def pack_unit(mask_poly, value_poly, key_row):
    cycle_width = mask_poly.shape[0]
    section_table = key_row.reshape(LEVELS, DIGITS, 2, cycle_width)
    for section_index in range(LEVELS):
        galois = cycle_width // (2 ** section_index) + 1
        mask_poly, value_poly = switch_section(mask_poly, value_poly, section_table[section_index], galois)
    return jnp.stack([mask_poly, value_poly])


def reference(database, queries, key_rows, hint, assignment):
    answers = jnp.dot(queries, database, preferred_element_type=jnp.int32)
    unit_rows = answers.reshape(CLIENTS * POLYS, CYCLE)

    def pack_one(unit_index):
        client = unit_index // POLYS
        poly_index = unit_index % POLYS
        mask_poly = lax.dynamic_index_in_dim(hint, poly_index, 0, keepdims=False)
        value_poly = lax.dynamic_index_in_dim(unit_rows, unit_index, 0, keepdims=False)
        key_row = lax.dynamic_index_in_dim(key_rows, client, 0, keepdims=False)
        return pack_unit(mask_poly, value_poly, key_row)

    packed_words = lax.map(pack_one, assignment)
    return packed_words.astype(jnp.float32) * (2.0 ** -32)
```

```python
import functools

import jax
import jax.numpy as jnp
from jax import lax
from jax.experimental import pallas as pl
from jax.experimental.pallas import tpu as pltpu
from jax.sharding import PartitionSpec as P

LEVELS = 2
DIGITS = 2
LANES = 128
DEPTH = 64


def step_masks(n):
    return [1] + [(1 << k) | 1 for k in range(1, n.bit_length() - 1)]


def row_masks(masks):
    rows = [0]
    for mask in reversed(masks):
        rows = rows + [r ^ mask for r in rows]
    return rows


def answer_kernel(n, polys, assignment, database, queries, key_rows, answers_out, keys_out, rows, key_scratch):
    clients = queries.shape[0]
    blocks = database.shape[1] // LANES
    cycle_blocks = blocks // polys
    words = queries[...]
    bytes_ = [jnp.bitwise_and(jnp.right_shift(words, 8 * j), 255) for j in range(4)]
    lhs = jnp.concatenate(bytes_, axis=0).astype(jnp.float32).astype(jnp.bfloat16)
    rhs = database[...].astype(jnp.float32).astype(jnp.bfloat16)
    sums = jnp.dot(lhs, rhs, preferred_element_type=jnp.float32).astype(jnp.int32)
    partial = sums[:clients]
    for j in range(1, 4):
        partial = partial + jnp.left_shift(sums[j * clients : (j + 1) * clients], 8 * j)
    for m in range(blocks):
        rows[pl.ds(m, clients, stride=blocks), :] = partial[:, m * LANES : (m + 1) * LANES]
    me = lax.axis_index("col")
    chunk = 0
    if keys_out is not None:
        chunk = key_rows.shape[1] // LANES
        for m in range(chunk):
            key_scratch[pl.ds(m, clients, stride=chunk), :] = key_rows[:, m * LANES : (m + 1) * LANES]
    for r, mask in enumerate(row_masks(step_masks(n))):
        unit = assignment[jnp.bitwise_xor(me, mask)]
        answers_out[r * cycle_blocks : (r + 1) * cycle_blocks, :] = rows[
            pl.ds(pl.multiple_of(unit * cycle_blocks, cycle_blocks), cycle_blocks), :
        ]
        if keys_out is not None:
            keys_out[r * chunk : (r + 1) * chunk, :] = key_scratch[pl.ds(unit // polys * chunk, chunk), :]


def shift_blocks(poly, count):
    blocks = poly.shape[0]
    whole, part = divmod(count % (2 * blocks), blocks)
    if part:
        row = lax.broadcasted_iota(jnp.int32, poly.shape, 0)
        poly = pltpu.roll(poly, part, 0)
        poly = jnp.where(row < part, -poly, poly)
    return -poly if whole else poly


def automorph(poly, level):
    blocks, lanes = poly.shape
    lane = lax.broadcasted_iota(jnp.int32, poly.shape, 1)
    period = 2 ** (level + 1)
    residue = jnp.bitwise_and(lane, period - 1)
    result = poly
    for m in range(1, period):
        result = jnp.where(residue == m, shift_blocks(poly, m * blocks // 2**level), result)
    return result


def toeplitz(word):
    blocks = word.shape[0]
    row = lax.broadcasted_iota(jnp.int32, (DEPTH, LANES), 0)
    lane = lax.broadcasted_iota(jnp.int32, (DEPTH, LANES), 1)
    inside = lane >= row
    turned = [
        pltpu.roll(jnp.broadcast_to(word[b : b + 1, :], (DEPTH, LANES)), 0, 1, stride=1, stride_axis=0)
        for b in range(blocks)
    ]
    columns = []
    for b in range(blocks):
        words = jnp.where(inside, turned[b], turned[b - 1])
        parts = []
        for j in range(4):
            part = jnp.bitwise_and(jnp.right_shift(words, 8 * j), 255).astype(jnp.float32)
            if b == 0:
                part = jnp.where(inside, part, -part)
            parts.append(part.astype(jnp.bfloat16))
        columns.append(jnp.concatenate(parts, axis=0))
    return jnp.concatenate(columns, axis=1)


def key_matrix(keys):
    lane = lax.broadcasted_iota(jnp.int32, keys[0][0].shape, 1)
    low = lane < DEPTH
    halves = [[None] * DIGITS for _ in range(4)]
    for p in range(2):
        for t in range(DIGITS):
            word = keys[t][p]
            other = pltpu.roll(word, DEPTH, 1)
            halves[2 * p][t] = jnp.where(low, word, jnp.left_shift(other, 8))
            halves[2 * p + 1][t] = jnp.where(low, other, jnp.left_shift(word, 8))
    rows = []
    for p in range(2):
        for s in range(4):
            for h in range(2):
                cut = [jnp.bitwise_and(jnp.right_shift(halves[2 * p + h][t], 8 * s), 255) for t in range(DIGITS)]
                rows.append(jnp.concatenate(cut, axis=1))
    return jnp.concatenate(rows, axis=0).astype(jnp.float32).astype(jnp.bfloat16)


def switch(keys, word):
    blocks = word.shape[0]
    sums = jnp.dot(key_matrix(keys), toeplitz(word), preferred_element_type=jnp.float32).astype(jnp.int32)
    lane = lax.broadcasted_iota(jnp.int32, word.shape, 1)
    results = []
    for p in range(2):
        halves = []
        for h in range(2):
            total = None
            for m in range(blocks):
                joined = None
                for s in range(4):
                    first = ((p * 4 + s) * 2 + h) * blocks
                    piece = jnp.left_shift(sums[first : first + blocks, m * LANES : (m + 1) * LANES], 8 * s)
                    joined = piece if joined is None else joined + piece
                moved = shift_blocks(joined, m)
                total = moved if total is None else total + moved
            halves.append(total)
        turned = pltpu.roll(halves[1], DEPTH, 1)
        results.append(halves[0] + jnp.where(lane < DEPTH, shift_blocks(turned, 1), turned))
    return results


def pack_kernel(n, polys, assignment, hint, answers, key_chunks, packed, keys):
    me = lax.axis_index("col")
    cycle_blocks = answers.shape[0]
    unit = assignment[me]
    mask = hint[unit % polys]
    value = answers[...]
    if len(key_chunks.shape) == 3:
        chunk = key_chunks.shape[1]
        order = row_masks(step_masks(n))
        for source in range(n):
            away = jnp.bitwise_xor(me, source)
            parity = away
            k = 1
            while k < n.bit_length():
                parity = jnp.bitwise_xor(parity, jnp.right_shift(parity, k))
                k *= 2
            slot = jnp.bitwise_or(jnp.bitwise_and(away, n - 2), jnp.bitwise_and(parity, 1))
            keys[source * chunk : (source + 1) * chunk, :] = key_chunks[slot]
    else:
        keys[...] = key_chunks[...]
    for level in range(LEVELS):
        table = [
            [keys[pl.ds(((level * DIGITS + t) * 2 + p) * cycle_blocks, cycle_blocks), :] for p in range(2)]
            for t in range(DIGITS)
        ]
        change = switch(table, automorph(mask, level))
        mask = mask + change[0]
        value = value + automorph(value, level) + change[1]
    for p, words in enumerate((mask, value)):
        scaled = words.astype(jnp.float32) * 2.0**-32
        for b in range(cycle_blocks):
            packed[0, p : p + 1, b * LANES : (b + 1) * LANES] = scaled[b : b + 1, :]


def on_device(database, queries, key_rows, hint, assignment):
    n = lax.axis_size("col")
    polys, cycle_width = hint.shape
    clients = queries.shape[0]
    cycle_blocks = cycle_width // LANES
    key_width = key_rows.shape[1]
    whole_rows = key_width % LANES == 0
    me = lax.axis_index("col")
    masks = step_masks(n)
    vmem = pl.BlockSpec(memory_space=pltpu.VMEM)
    smem = pl.BlockSpec(memory_space=pltpu.SMEM)
    chunk = key_width // LANES

    out_shape = [jax.ShapeDtypeStruct((n * cycle_blocks, LANES), jnp.int32)]
    if whole_rows:
        out_shape.append(jax.ShapeDtypeStruct((n * chunk, LANES), jnp.int32))

        def first_kernel(*refs):
            answer_kernel(n, polys, *refs)
    else:

        def first_kernel(assignment, database, queries, key_rows, answers_out, rows, key_scratch):
            answer_kernel(n, polys, assignment, database, queries, key_rows, answers_out, None, rows, key_scratch)

    outs = pl.pallas_call(
        first_kernel,
        out_shape=out_shape,
        in_specs=[smem, vmem, vmem, vmem],
        out_specs=[vmem] * len(out_shape),
        scratch_shapes=[
            pltpu.VMEM((clients * polys * cycle_blocks, LANES), jnp.int32),
            pltpu.VMEM((clients * max(chunk, 1), LANES), jnp.int32),
        ],
    )(assignment, database, queries, key_rows)
    answers = outs[0].reshape(n, cycle_blocks, LANES)
    if whole_rows:
        keys = outs[1].reshape(1, n, chunk, LANES)
    else:
        order = jnp.bitwise_xor(jnp.array(row_masks(masks), jnp.int32), me)
        keys = jnp.take(key_rows, assignment[order] // polys, axis=0).reshape(1, n, 1, key_width)

    rows = n
    for mask in masks:
        half = rows // 2
        sent = jnp.concatenate(
            [answers[half:].reshape(-1, LANES), keys[:, half:].reshape(-1, LANES)], axis=0
        )
        got = lax.ppermute(sent, "col", [(i, i ^ mask) for i in range(n)])
        answers = answers[:half] + got[: half * cycle_blocks].reshape(half, cycle_blocks, LANES)
        kept = keys[:, :half]
        keys = jnp.concatenate([kept, got[half * cycle_blocks :].reshape(kept.shape)], axis=0)
        rows = half

    answers = answers.reshape(cycle_blocks, LANES)
    if whole_rows:
        keys = keys.reshape(n, chunk, LANES)
    else:
        away = jnp.bitwise_xor(jnp.arange(n, dtype=jnp.int32), me)
        parity = away
        k = 1
        while k < n.bit_length():
            parity = jnp.bitwise_xor(parity, jnp.right_shift(parity, k))
            k *= 2
        slot = jnp.bitwise_or(jnp.bitwise_and(away, n - 2), jnp.bitwise_and(parity, 1))
        keys = jnp.take(keys.reshape(n, key_width), slot, axis=0).reshape(-1, LANES)

    return pl.pallas_call(
        functools.partial(pack_kernel, n, polys),
        out_shape=jax.ShapeDtypeStruct((1, 2, cycle_width), jnp.float32),
        in_specs=[smem, vmem, vmem, vmem],
        out_specs=vmem,
        scratch_shapes=[pltpu.VMEM((LEVELS * DIGITS * 2 * cycle_blocks, LANES), jnp.int32)],
    )(assignment, hint.reshape(polys, cycle_blocks, LANES), answers, keys)


def solution(mesh):
    placed = (P("col", "grp"), P("grp", "col"), P("grp", "col"), P("grp", None), P("grp"))
    return jax.shard_map(
        on_device,
        mesh=mesh,
        in_specs=placed,
        out_specs=P(("grp", "col"), None, None),
        check_vma=False,
    )
```

```python
import functools

import jax
import jax.numpy as jnp
from jax import lax
from jax.experimental import pallas as pl
from jax.experimental.pallas import tpu as pltpu
from jax.sharding import PartitionSpec as P

LEVELS = 2
DIGITS = 2
LANES = 128
DEPTH = 64


def step_masks(n):
    return [1] + [(1 << k) | 1 for k in range(1, n.bit_length() - 1)]


def row_masks(masks):
    rows = [0]
    for mask in reversed(masks):
        rows = rows + [r ^ mask for r in rows]
    return rows


def answer_kernel(n, polys, assignment, database, queries, key_rows, kept, sent, rows, key_scratch):
    clients = queries.shape[0]
    blocks = database.shape[1] // LANES
    cycle_blocks = blocks // polys
    words = queries[...]
    bytes_ = [jnp.bitwise_and(jnp.right_shift(words, 8 * j), 255) for j in range(4)]
    lhs = jnp.concatenate(bytes_, axis=0).astype(jnp.float32).astype(jnp.bfloat16)
    rhs = database[...].astype(jnp.float32).astype(jnp.bfloat16)
    sums = jnp.dot(lhs, rhs, preferred_element_type=jnp.float32).astype(jnp.int32)
    partial = sums[:clients]
    for j in range(1, 4):
        partial = partial + jnp.left_shift(sums[j * clients : (j + 1) * clients], 8 * j)
    for m in range(blocks):
        rows[pl.ds(m, clients, stride=blocks), :] = partial[:, m * LANES : (m + 1) * LANES]
    half = n // 2
    chunk = kept.shape[0] // half - cycle_blocks
    for m in range(chunk):
        key_scratch[pl.ds(m, clients, stride=chunk), :] = key_rows[:, m * LANES : (m + 1) * LANES]
    me = lax.axis_index("col")
    for r, mask in enumerate(row_masks(step_masks(n))):
        unit = assignment[jnp.bitwise_xor(me, mask)]
        out, place = (kept, r) if r < half else (sent, r - half)
        out[place * cycle_blocks : (place + 1) * cycle_blocks, :] = rows[
            pl.ds(pl.multiple_of(unit * cycle_blocks, cycle_blocks), cycle_blocks), :
        ]
        if chunk:
            place = half * cycle_blocks + place * chunk
            out[place : place + chunk, :] = key_scratch[pl.ds(unit // polys * chunk, chunk), :]


def join_kernel(cycle_blocks, rows, chunk, kept, got, next_kept, next_sent):
    half = rows // 2
    cut = half * cycle_blocks
    next_kept[:cut, :] = kept[:cut, :] + got[:cut, :]
    next_sent[:cut, :] = kept[cut : 2 * cut, :] + got[cut : 2 * cut, :]
    if chunk:
        sources = (kept.shape[0] - 2 * cut) // (rows * chunk)
        size = half * chunk
        for s in range(2 * sources):
            part = kept if s < sources else got
            first = 2 * cut + s % sources * 2 * size
            next_kept[cut + s * size : cut + (s + 1) * size, :] = part[first : first + size, :]
            next_sent[cut + s * size : cut + (s + 1) * size, :] = part[first + size : first + 2 * size, :]


def shift_blocks(poly, count):
    blocks = poly.shape[0]
    whole, part = divmod(count % (2 * blocks), blocks)
    if part:
        row = lax.broadcasted_iota(jnp.int32, poly.shape, 0)
        poly = pltpu.roll(poly, part, 0)
        poly = jnp.where(row < part, -poly, poly)
    return -poly if whole else poly


def automorph(poly, level):
    blocks, lanes = poly.shape
    lane = lax.broadcasted_iota(jnp.int32, poly.shape, 1)
    period = 2 ** (level + 1)
    residue = jnp.bitwise_and(lane, period - 1)
    result = poly
    for m in range(1, period):
        result = jnp.where(residue == m, shift_blocks(poly, m * blocks // 2**level), result)
    return result


def toeplitz(word):
    blocks = word.shape[0]
    row = lax.broadcasted_iota(jnp.int32, (DEPTH, LANES), 0)
    lane = lax.broadcasted_iota(jnp.int32, (DEPTH, LANES), 1)
    inside = lane >= row
    turned = [
        pltpu.roll(jnp.broadcast_to(word[b : b + 1, :], (DEPTH, LANES)), 0, 1, stride=1, stride_axis=0)
        for b in range(blocks)
    ]
    columns = []
    for b in range(blocks):
        words = jnp.where(inside, turned[b], turned[b - 1])
        parts = []
        for j in range(4):
            part = jnp.bitwise_and(jnp.right_shift(words, 8 * j), 255).astype(jnp.float32)
            if b == 0:
                part = jnp.where(inside, part, -part)
            parts.append(part.astype(jnp.bfloat16))
        columns.append(jnp.concatenate(parts, axis=0))
    return jnp.concatenate(columns, axis=1)


def key_matrix(keys):
    lane = lax.broadcasted_iota(jnp.int32, keys[0][0].shape, 1)
    low = lane < DEPTH
    halves = [[None] * DIGITS for _ in range(4)]
    for p in range(2):
        for t in range(DIGITS):
            word = keys[t][p]
            other = pltpu.roll(word, DEPTH, 1)
            halves[2 * p][t] = jnp.where(low, word, jnp.left_shift(other, 8))
            halves[2 * p + 1][t] = jnp.where(low, other, jnp.left_shift(word, 8))
    rows = []
    for p in range(2):
        for s in range(4):
            for h in range(2):
                cut = [jnp.bitwise_and(jnp.right_shift(halves[2 * p + h][t], 8 * s), 255) for t in range(DIGITS)]
                rows.append(jnp.concatenate(cut, axis=1))
    return jnp.concatenate(rows, axis=0).astype(jnp.float32).astype(jnp.bfloat16)


def switch(keys, digits, blocks):
    sums = jnp.dot(key_matrix(keys), digits, preferred_element_type=jnp.float32).astype(jnp.int32)
    lane = lax.broadcasted_iota(jnp.int32, (blocks, LANES), 1)
    results = []
    for p in range(2):
        halves = []
        for h in range(2):
            total = None
            for m in range(blocks):
                joined = None
                for s in range(4):
                    first = ((p * 4 + s) * 2 + h) * blocks
                    piece = jnp.left_shift(sums[first : first + blocks, m * LANES : (m + 1) * LANES], 8 * s)
                    joined = piece if joined is None else joined + piece
                moved = shift_blocks(joined, m)
                total = moved if total is None else total + moved
            halves.append(total)
        turned = pltpu.roll(halves[1], DEPTH, 1)
        results.append(halves[0] + jnp.where(lane < DEPTH, shift_blocks(turned, 1), turned))
    return results


def digit_kernel(polys, assignment, hint, mask_out, digits_out):
    cycle_blocks = mask_out.shape[0]
    poly = assignment[lax.axis_index("col")] % polys
    row = hint[pl.ds(poly, 1), :]
    mask = jnp.concatenate([row[:, b * LANES : (b + 1) * LANES] for b in range(cycle_blocks)], axis=0)
    mask_out[...] = mask
    digits_out[...] = toeplitz(automorph(mask, 0))


def pack_kernel(n, chunk, mask_in, digits, kept, got, *refs):
    if chunk:
        packed, stacked, keys = refs
    else:
        keys, packed = refs
    cycle_blocks = mask_in.shape[0]
    mask = mask_in[...]
    value = kept[:cycle_blocks, :] + got[:cycle_blocks, :]
    if chunk:
        stacked[: n // 2 * chunk, :] = kept[cycle_blocks:, :]
        stacked[n // 2 * chunk :, :] = got[cycle_blocks:, :]
        me = lax.axis_index("col")
        for source in range(n):
            slot = slot_of(n, jnp.bitwise_xor(me, source))
            keys[source * chunk : (source + 1) * chunk, :] = stacked[pl.ds(slot * chunk, chunk), :]
    for level in range(LEVELS):
        table = [
            [keys[pl.ds(((level * DIGITS + t) * 2 + p) * cycle_blocks, cycle_blocks), :] for p in range(2)]
            for t in range(DIGITS)
        ]
        change = switch(table, digits[...] if level == 0 else toeplitz(automorph(mask, level)), cycle_blocks)
        mask = mask + change[0]
        value = value + automorph(value, level) + change[1]
    for p, words in enumerate((mask, value)):
        scaled = words.astype(jnp.float32) * 2.0**-32
        for b in range(cycle_blocks):
            packed[0, p : p + 1, b * LANES : (b + 1) * LANES] = scaled[b : b + 1, :]


def slot_of(n, away):
    parity = away
    k = 1
    while k < n.bit_length():
        parity = jnp.bitwise_xor(parity, jnp.right_shift(parity, k))
        k *= 2
    return jnp.bitwise_or(jnp.bitwise_and(away, n - 2), jnp.bitwise_and(parity, 1))


def near(x):
    return pltpu.with_memory_space_constraint(x, pltpu.VMEM)


def on_device(database, queries, key_rows, hint, assignment):
    n = lax.axis_size("col")
    polys, cycle_width = hint.shape
    clients = queries.shape[0]
    cycle_blocks = cycle_width // LANES
    key_width = key_rows.shape[1]
    masks = step_masks(n)
    vmem = pl.BlockSpec(memory_space=pltpu.VMEM)
    smem = pl.BlockSpec(memory_space=pltpu.SMEM)
    chunk = key_width // LANES if key_width % LANES == 0 else 0
    units = clients * polys

    def exchange(x, mask):
        return lax.ppermute(x, "col", [(i, i ^ mask) for i in range(n)])

    rows = n // 2
    kept, sent = pl.pallas_call(
        functools.partial(answer_kernel, n, polys),
        out_shape=[pltpu.VMEM((rows * (cycle_blocks + chunk), LANES), jnp.int32)] * 2,
        in_specs=[smem, vmem, vmem, vmem],
        out_specs=[vmem] * 2,
        scratch_shapes=[
            pltpu.VMEM((units * cycle_blocks, LANES), jnp.int32),
            pltpu.VMEM((max(clients * chunk, 8), LANES), jnp.int32),
        ],
    )(assignment, database, queries, key_rows)
    mask_poly, digits = pl.pallas_call(
        functools.partial(digit_kernel, polys),
        out_shape=[
            pltpu.VMEM((cycle_blocks, LANES), jnp.int32),
            pltpu.VMEM((2 * DIGITS * DEPTH, cycle_width), jnp.bfloat16),
        ],
        in_specs=[smem, vmem],
        out_specs=[vmem] * 2,
    )(assignment, hint)

    for step, mask in enumerate(masks):
        got = exchange(sent, mask)
        if step < len(masks) - 1:
            half_rows = kept.shape[0] - rows // 2 * cycle_blocks if chunk else rows // 2 * cycle_blocks
            kept, sent = pl.pallas_call(
                functools.partial(join_kernel, cycle_blocks, rows, chunk),
                out_shape=[pltpu.VMEM((half_rows, LANES), jnp.int32)] * 2,
                in_specs=[vmem] * 2,
                out_specs=[vmem] * 2,
            )(near(kept), near(got))
            rows //= 2

    operands = [near(mask_poly), near(digits), near(kept), near(got)]
    if not chunk:
        me = lax.axis_index("col")
        order = jnp.bitwise_xor(jnp.array(row_masks(masks), jnp.int32), me)
        keys = jnp.take(key_rows, assignment[order] // polys, axis=0)[None]
        for mask in masks:
            half = keys.shape[1] // 2
            keys = jnp.concatenate([keys[:, :half], exchange(keys[:, half:], mask)], axis=0)
        slots = slot_of(n, jnp.bitwise_xor(jnp.arange(n, dtype=jnp.int32), me))
        operands.append(jnp.take(keys.reshape(n, key_width), slots, axis=0).reshape(-1, LANES))
    return pl.pallas_call(
        functools.partial(pack_kernel, n, chunk),
        out_shape=jax.ShapeDtypeStruct((1, 2, cycle_width), jnp.float32),
        in_specs=[vmem] * len(operands),
        out_specs=vmem,
        scratch_shapes=[pltpu.VMEM((n * chunk, LANES), jnp.int32)] * 2 if chunk else [],
    )(*operands)


def solution(mesh):
    placed = (P("col", "grp"), P("grp", "col"), P("grp", "col"), P("grp", None), P("grp"))
    return jax.shard_map(
        on_device,
        mesh=mesh,
        in_specs=placed,
        out_specs=P(("grp", "col"), None, None),
        check_vma=False,
    )
```

```python
import functools

import jax
import jax.numpy as jnp
from jax import lax
from jax.experimental import pallas as pl
from jax.experimental.pallas import tpu as pltpu
from jax.sharding import PartitionSpec as P

LEVELS = 2
DIGITS = 2
LANES = 128
DEPTH = 64


def stages_of(n):
    bits = [1 << k for k in range(n.bit_length() - 1)]
    pair = [bits[1] | bits[2] | 1, bits[2] | 1, bits[1] | 1] if len(bits) > 2 else [b | 1 for b in bits[1:2]]
    return [[1]] + [pair] * (len(pair) > 0) + [[b | 1] for b in bits[3:]]


def destinations(stages):
    rows = [0]
    for stage in reversed(stages):
        rows = [r ^ mask for mask in [0] + stage for r in rows]
    return rows


def sources(stages):
    return destinations(stages[::-1])


def answer_kernel(n, polys, assignment, database, queries, key_rows, *refs):
    outs, (rows, key_scratch) = refs[:-2], refs[-2:]
    clients = queries.shape[0]
    blocks = database.shape[1] // LANES
    cycle_blocks = blocks // polys
    words = queries[...]
    bytes_ = [jnp.bitwise_and(jnp.right_shift(words, 8 * j), 255) for j in range(4)]
    lhs = jnp.concatenate(bytes_, axis=0).astype(jnp.float32).astype(jnp.bfloat16)
    rhs = database[...].astype(jnp.float32).astype(jnp.bfloat16)
    sums = jnp.dot(lhs, rhs, preferred_element_type=jnp.float32).astype(jnp.int32)
    partial = sums[:clients]
    for j in range(1, 4):
        partial = partial + jnp.left_shift(sums[j * clients : (j + 1) * clients], 8 * j)
    for m in range(blocks):
        rows[pl.ds(m, clients, stride=blocks), :] = partial[:, m * LANES : (m + 1) * LANES]
    share = n // len(outs)
    chunk = outs[0].shape[0] // share - cycle_blocks
    for m in range(chunk):
        key_scratch[pl.ds(m, clients, stride=chunk), :] = key_rows[:, m * LANES : (m + 1) * LANES]
    me = lax.axis_index("col")
    for r, mask in enumerate(destinations(stages_of(n))):
        unit = assignment[jnp.bitwise_xor(me, mask)]
        out, place = outs[r // share], r % share
        out[place * cycle_blocks : (place + 1) * cycle_blocks, :] = rows[
            pl.ds(pl.multiple_of(unit * cycle_blocks, cycle_blocks), cycle_blocks), :
        ]
        if chunk:
            first = share * cycle_blocks + place * chunk
            out[first : first + chunk, :] = key_scratch[pl.ds(unit // polys * chunk, chunk), :]


def join_kernel(cycle_blocks, rows, chunk, partners, *refs):
    parts, outs = refs[:partners], refs[partners:]
    share = rows // len(outs)
    cut = rows * cycle_blocks
    size = share * chunk
    for o, out in enumerate(outs):
        span = slice(o * share * cycle_blocks, (o + 1) * share * cycle_blocks)
        total = parts[0][span, :]
        for part in parts[1:]:
            total = total + part[span, :]
        out[: share * cycle_blocks, :] = total
        if chunk:
            stacked = (parts[0].shape[0] - cut) // (rows * chunk)
            for s in range(stacked * partners):
                source = cut + (s % stacked) * rows * chunk + o * size
                target = share * cycle_blocks + s * size
                out[target : target + size, :] = parts[s // stacked][source : source + size, :]


def shift_blocks(poly, count):
    blocks = poly.shape[0]
    whole, part = divmod(count % (2 * blocks), blocks)
    if part:
        row = lax.broadcasted_iota(jnp.int32, poly.shape, 0)
        poly = pltpu.roll(poly, part, 0)
        poly = jnp.where(row < part, -poly, poly)
    return -poly if whole else poly


def automorph(poly, level):
    blocks, lanes = poly.shape
    lane = lax.broadcasted_iota(jnp.int32, poly.shape, 1)
    period = 2 ** (level + 1)
    residue = jnp.bitwise_and(lane, period - 1)
    result = poly
    for m in range(1, period):
        result = jnp.where(residue == m, shift_blocks(poly, m * blocks // 2**level), result)
    return result


def toeplitz(word):
    blocks = word.shape[0]
    row = lax.broadcasted_iota(jnp.int32, (DEPTH, LANES), 0)
    lane = lax.broadcasted_iota(jnp.int32, (DEPTH, LANES), 1)
    inside = lane >= row
    turned = [
        pltpu.roll(jnp.broadcast_to(word[b : b + 1, :], (DEPTH, LANES)), 0, 1, stride=1, stride_axis=0)
        for b in range(blocks)
    ]
    columns = []
    for b in range(blocks):
        words = jnp.where(inside, turned[b], turned[b - 1])
        parts = []
        for j in range(4):
            part = jnp.bitwise_and(jnp.right_shift(words, 8 * j), 255).astype(jnp.float32)
            if b == 0:
                part = jnp.where(inside, part, -part)
            parts.append(part.astype(jnp.bfloat16))
        columns.append(jnp.concatenate(parts, axis=0))
    return jnp.concatenate(columns, axis=1)


def key_matrix(keys):
    lane = lax.broadcasted_iota(jnp.int32, keys[0][0].shape, 1)
    low = lane < DEPTH
    halves = [[None] * DIGITS for _ in range(4)]
    for p in range(2):
        for t in range(DIGITS):
            word = keys[t][p]
            other = pltpu.roll(word, DEPTH, 1)
            halves[2 * p][t] = jnp.where(low, word, jnp.left_shift(other, 8))
            halves[2 * p + 1][t] = jnp.where(low, other, jnp.left_shift(word, 8))
    rows = []
    for p in range(2):
        for s in range(4):
            for h in range(2):
                cut = [jnp.bitwise_and(jnp.right_shift(halves[2 * p + h][t], 8 * s), 255) for t in range(DIGITS)]
                rows.append(jnp.concatenate(cut, axis=1))
    return jnp.concatenate(rows, axis=0).astype(jnp.float32).astype(jnp.bfloat16)


def switch(keys, digits, blocks):
    sums = jnp.dot(key_matrix(keys), digits, preferred_element_type=jnp.float32).astype(jnp.int32)
    lane = lax.broadcasted_iota(jnp.int32, (blocks, LANES), 1)
    results = []
    for p in range(2):
        halves = []
        for h in range(2):
            total = None
            for m in range(blocks):
                joined = None
                for s in range(4):
                    first = ((p * 4 + s) * 2 + h) * blocks
                    piece = jnp.left_shift(sums[first : first + blocks, m * LANES : (m + 1) * LANES], 8 * s)
                    joined = piece if joined is None else joined + piece
                moved = shift_blocks(joined, m)
                total = moved if total is None else total + moved
            halves.append(total)
        turned = pltpu.roll(halves[1], DEPTH, 1)
        results.append(halves[0] + jnp.where(lane < DEPTH, shift_blocks(turned, 1), turned))
    return results


def digit_kernel(polys, assignment, hint, mask_out, digits_out):
    cycle_blocks = mask_out.shape[0]
    poly = assignment[lax.axis_index("col")] % polys
    row = hint[pl.ds(poly, 1), :]
    mask = jnp.concatenate([row[:, b * LANES : (b + 1) * LANES] for b in range(cycle_blocks)], axis=0)
    mask_out[...] = mask
    digits_out[...] = toeplitz(automorph(mask, 0))


def pack_kernel(n, chunk, partners, mask_in, digits, *refs):
    parts = refs[:partners]
    packed, keys = refs[partners:] if chunk else refs[:partners - 1 : -1]
    cycle_blocks = mask_in.shape[0]
    mask = mask_in[...]
    value = parts[0][:cycle_blocks, :]
    for part in parts[1:]:
        value = value + part[:cycle_blocks, :]
    if chunk:
        me = lax.axis_index("col")
        stacked = n // partners
        for slot, away in enumerate(sources(stages_of(n))):
            first = cycle_blocks + slot % stacked * chunk
            keys[pl.ds(jnp.bitwise_xor(me, away) * chunk, chunk), :] = parts[slot // stacked][first : first + chunk, :]
    for level in range(LEVELS):
        table = [
            [keys[pl.ds(((level * DIGITS + t) * 2 + p) * cycle_blocks, cycle_blocks), :] for p in range(2)]
            for t in range(DIGITS)
        ]
        change = switch(table, digits[...] if level == 0 else toeplitz(automorph(mask, level)), cycle_blocks)
        mask = mask + change[0]
        value = value + automorph(value, level) + change[1]
    for p, words in enumerate((mask, value)):
        scaled = words.astype(jnp.float32) * 2.0**-32
        for b in range(cycle_blocks):
            packed[0, p : p + 1, b * LANES : (b + 1) * LANES] = scaled[b : b + 1, :]


def near(x):
    return pltpu.with_memory_space_constraint(x, pltpu.VMEM)


def on_device(database, queries, key_rows, hint, assignment):
    n = lax.axis_size("col")
    polys, cycle_width = hint.shape
    clients = queries.shape[0]
    cycle_blocks = cycle_width // LANES
    key_width = key_rows.shape[1]
    stages = stages_of(n)
    vmem = pl.BlockSpec(memory_space=pltpu.VMEM)
    smem = pl.BlockSpec(memory_space=pltpu.SMEM)
    chunk = key_width // LANES if key_width % LANES == 0 else 0

    def exchange(x, mask):
        return lax.ppermute(x, "col", [(i, i ^ mask) for i in range(n)])

    pieces = len(stages[0]) + 1
    rows = n // pieces
    parts = pl.pallas_call(
        functools.partial(answer_kernel, n, polys),
        out_shape=[pltpu.VMEM((rows * (cycle_blocks + chunk), LANES), jnp.int32)] * pieces,
        in_specs=[smem, vmem, vmem, vmem],
        out_specs=[vmem] * pieces,
        scratch_shapes=[
            pltpu.VMEM((clients * polys * cycle_blocks, LANES), jnp.int32),
            pltpu.VMEM((max(clients * chunk, 8), LANES), jnp.int32),
        ],
    )(assignment, database, queries, key_rows)
    mask_poly, digits = pl.pallas_call(
        functools.partial(digit_kernel, polys),
        out_shape=[
            pltpu.VMEM((cycle_blocks, LANES), jnp.int32),
            pltpu.VMEM((2 * DIGITS * DEPTH, cycle_width), jnp.bfloat16),
        ],
        in_specs=[smem, vmem],
        out_specs=[vmem] * 2,
    )(assignment, hint)

    stacked = 1
    for step, stage in enumerate(stages):
        parts = [parts[0]] + [exchange(part, mask) for part, mask in zip(parts[1:], stage)]
        stacked *= len(parts)
        if step < len(stages) - 1:
            pieces = len(stages[step + 1]) + 1
            share = rows // pieces
            parts = pl.pallas_call(
                functools.partial(join_kernel, cycle_blocks, rows, chunk, len(parts)),
                out_shape=[pltpu.VMEM((share * (cycle_blocks + stacked * chunk), LANES), jnp.int32)] * pieces,
                in_specs=[vmem] * len(parts),
                out_specs=[vmem] * pieces,
            )(*map(near, parts))
            rows = share

    operands = [near(x) for x in (mask_poly, digits, *parts)]
    if not chunk:
        me = lax.axis_index("col")
        order = jnp.bitwise_xor(jnp.array(destinations(stages), jnp.int32), me)
        keys = jnp.take(key_rows, assignment[order] // polys, axis=0)[None]
        for stage in stages:
            cuts = jnp.split(keys, len(stage) + 1, axis=1)
            keys = jnp.concatenate([cuts[0]] + [exchange(x, mask) for x, mask in zip(cuts[1:], stage)], axis=0)
        away = sources(stages)
        places = jnp.array([away.index(i) for i in range(n)], jnp.int32)
        places = places[jnp.bitwise_xor(jnp.arange(n, dtype=jnp.int32), me)]
        operands.append(jnp.take(keys.reshape(n, key_width), places, axis=0).reshape(-1, LANES))
    return pl.pallas_call(
        functools.partial(pack_kernel, n, chunk, len(parts)),
        out_shape=jax.ShapeDtypeStruct((1, 2, cycle_width), jnp.float32),
        in_specs=[vmem] * len(operands),
        out_specs=vmem,
        scratch_shapes=[pltpu.VMEM((n * chunk, LANES), jnp.int32)] if chunk else [],
    )(*operands)


def solution(mesh):
    placed = (P("col", "grp"), P("grp", "col"), P("grp", "col"), P("grp", None), P("grp"))
    return jax.shard_map(
        on_device,
        mesh=mesh,
        in_specs=placed,
        out_specs=P(("grp", "col"), None, None),
        check_vma=False,
    )
```

```python
import functools

import jax
import jax.numpy as jnp
from jax import lax
from jax.experimental import pallas as pl
from jax.experimental.pallas import tpu as pltpu
from jax.sharding import PartitionSpec as P

LEVELS = 2
DIGITS = 2
LANES = 128
DEPTH = 64


def stages_of(n):
    bits = [1 << k for k in range(n.bit_length() - 1)]
    pair = [bits[1] | bits[2] | 1, bits[2] | 1, bits[1] | 1] if len(bits) > 2 else [b | 1 for b in bits[1:2]]
    return [[1]] + [pair] * (len(pair) > 0) + [[b | 1] for b in bits[3:]]


def destinations(stages):
    rows = [0]
    for stage in reversed(stages):
        rows = [r ^ mask for mask in [0] + stage for r in rows]
    return rows


def sources(stages):
    return destinations(stages[::-1])


def answer_kernel(n, polys, assignment, database, queries, key_rows, *refs):
    outs, (rows, key_scratch) = refs[:-2], refs[-2:]
    clients = queries.shape[0]
    blocks = database.shape[1] // LANES
    cycle_blocks = blocks // polys
    words = queries[...]
    bytes_ = [jnp.bitwise_and(jnp.right_shift(words, 8 * j), 255) for j in range(4)]
    lhs = jnp.concatenate(bytes_, axis=0).astype(jnp.float32).astype(jnp.bfloat16)
    rhs = database[...].astype(jnp.float32).astype(jnp.bfloat16)
    sums = jnp.dot(lhs, rhs, preferred_element_type=jnp.float32).astype(jnp.int32)
    partial = sums[:clients]
    for j in range(1, 4):
        partial = partial + jnp.left_shift(sums[j * clients : (j + 1) * clients], 8 * j)
    for m in range(blocks):
        rows[pl.ds(m, clients, stride=blocks), :] = partial[:, m * LANES : (m + 1) * LANES]
    share = n // len(outs)
    chunk = outs[0].shape[0] // share - cycle_blocks
    for m in range(chunk):
        key_scratch[pl.ds(m, clients, stride=chunk), :] = key_rows[:, m * LANES : (m + 1) * LANES]
    me = lax.axis_index("col")
    for r, mask in enumerate(destinations(stages_of(n))):
        unit = assignment[jnp.bitwise_xor(me, mask)]
        out, place = outs[r // share], r % share
        out[place * cycle_blocks : (place + 1) * cycle_blocks, :] = rows[
            pl.ds(pl.multiple_of(unit * cycle_blocks, cycle_blocks), cycle_blocks), :
        ]
        if chunk:
            first = share * cycle_blocks + place * chunk
            out[first : first + chunk, :] = key_scratch[pl.ds(unit // polys * chunk, chunk), :]


def join_kernel(cycle_blocks, rows, chunk, partners, *refs):
    parts, outs = refs[:partners], refs[partners:]
    share = rows // len(outs)
    cut = rows * cycle_blocks
    size = share * chunk
    for o, out in enumerate(outs):
        span = slice(o * share * cycle_blocks, (o + 1) * share * cycle_blocks)
        total = parts[0][span, :]
        for part in parts[1:]:
            total = total + part[span, :]
        out[: share * cycle_blocks, :] = total
        if chunk:
            stacked = (parts[0].shape[0] - cut) // (rows * chunk)
            for s in range(stacked * partners):
                source = cut + (s % stacked) * rows * chunk + o * size
                target = share * cycle_blocks + s * size
                out[target : target + size, :] = parts[s // stacked][source : source + size, :]


def shift_blocks(poly, count):
    blocks = poly.shape[0]
    whole, part = divmod(count % (2 * blocks), blocks)
    if part:
        row = lax.broadcasted_iota(jnp.int32, poly.shape, 0)
        poly = pltpu.roll(poly, part, 0)
        poly = jnp.where(row < part, -poly, poly)
    return -poly if whole else poly


def automorph(poly, level):
    blocks, lanes = poly.shape
    lane = lax.broadcasted_iota(jnp.int32, poly.shape, 1)
    period = 2 ** (level + 1)
    residue = jnp.bitwise_and(lane, period - 1)
    result = poly
    for m in range(1, period):
        result = jnp.where(residue == m, shift_blocks(poly, m * blocks // 2**level), result)
    return result


def toeplitz(word):
    blocks = word.shape[0]
    row = lax.broadcasted_iota(jnp.int32, (DEPTH, LANES), 0)
    lane = lax.broadcasted_iota(jnp.int32, (DEPTH, LANES), 1)
    inside = lane >= row
    turned = [
        pltpu.roll(jnp.broadcast_to(word[b : b + 1, :], (DEPTH, LANES)), 0, 1, stride=1, stride_axis=0)
        for b in range(blocks)
    ]
    columns = []
    for b in range(blocks):
        words = jnp.where(inside, turned[b], turned[b - 1])
        parts = []
        for j in range(4):
            part = jnp.bitwise_and(jnp.right_shift(words, 8 * j), 255).astype(jnp.float32)
            if b == 0:
                part = jnp.where(inside, part, -part)
            parts.append(part.astype(jnp.bfloat16))
        columns.append(jnp.concatenate(parts, axis=0))
    return jnp.concatenate(columns, axis=1)


def key_matrix(keys):
    lane = lax.broadcasted_iota(jnp.int32, keys[0][0].shape, 1)
    low = lane < DEPTH
    halves = [[None] * DIGITS for _ in range(4)]
    for p in range(2):
        for t in range(DIGITS):
            word = keys[t][p]
            other = pltpu.roll(word, DEPTH, 1)
            halves[2 * p][t] = jnp.where(low, word, jnp.left_shift(other, 8))
            halves[2 * p + 1][t] = jnp.where(low, other, jnp.left_shift(word, 8))
    rows = []
    for p in range(2):
        for s in range(4):
            for h in range(2):
                cut = [jnp.bitwise_and(jnp.right_shift(halves[2 * p + h][t], 8 * s), 255) for t in range(DIGITS)]
                rows.append(jnp.concatenate(cut, axis=1))
    return jnp.concatenate(rows, axis=0).astype(jnp.float32).astype(jnp.bfloat16)


def switch(keys, digits, blocks):
    sums = jnp.dot(key_matrix(keys), digits, preferred_element_type=jnp.float32).astype(jnp.int32)
    lane = lax.broadcasted_iota(jnp.int32, (blocks, LANES), 1)
    results = []
    for p in range(2):
        halves = []
        for h in range(2):
            total = None
            for m in range(blocks):
                joined = None
                for s in range(4):
                    first = ((p * 4 + s) * 2 + h) * blocks
                    piece = jnp.left_shift(sums[first : first + blocks, m * LANES : (m + 1) * LANES], 8 * s)
                    joined = piece if joined is None else joined + piece
                moved = shift_blocks(joined, m)
                total = moved if total is None else total + moved
            halves.append(total)
        turned = pltpu.roll(halves[1], DEPTH, 1)
        results.append(halves[0] + jnp.where(lane < DEPTH, shift_blocks(turned, 1), turned))
    return results


def digit_kernel(polys, assignment, hint, mask_out, digits_out):
    cycle_blocks = mask_out.shape[0]
    poly = assignment[lax.axis_index("col")] % polys
    row = hint[pl.ds(poly, 1), :]
    mask = jnp.concatenate([row[:, b * LANES : (b + 1) * LANES] for b in range(cycle_blocks)], axis=0)
    mask_out[...] = mask
    digits_out[...] = toeplitz(automorph(mask, 0))


def holds_first(n, stages):
    return jnp.logical_and(lax.axis_index("col") < n // 2, stages[-1] == [n // 2 + 1])


def key_table(keys, level, cycle_blocks):
    return [
        [keys[pl.ds(((level * DIGITS + t) * 2 + p) * cycle_blocks, cycle_blocks), :] for p in range(2)]
        for t in range(DIGITS)
    ]


def place_keys(n, chunk, cycle_blocks, away, part, keys):
    me = lax.axis_index("col")
    for slot, distance in enumerate(away):
        first = cycle_blocks + slot * chunk
        keys[pl.ds(jnp.bitwise_xor(me, distance) * chunk, chunk), :] = part[first : first + chunk, :]


def early_kernel(n, chunk, mask_in, digits_in, part, mask_out, change_out, digits_out, keys):
    stages = stages_of(n)
    early = holds_first(n, stages)
    cycle_blocks = mask_in.shape[0]

    @pl.when(early)
    def _():
        place_keys(n, chunk, cycle_blocks, sources(stages[:-1]), part, keys)
        change = switch(key_table(keys, 0, cycle_blocks), digits_in[...], cycle_blocks)
        mask = mask_in[...] + change[0]
        mask_out[...] = mask
        change_out[...] = change[1]
        digits_out[...] = toeplitz(automorph(mask, 1))

    @pl.when(jnp.logical_not(early))
    def _():
        mask_out[...] = mask_in[...]
        change_out[...] = jnp.zeros_like(change_out)
        digits_out[...] = digits_in[...]


def pack_kernel(n, chunk, partners, mask_in, digits, *refs):
    cycle_blocks = mask_in.shape[0]
    stages = stages_of(n)
    if chunk:
        change_in, *parts, packed, keys = refs
        stacked = n // partners
        away = sources(stages)
        for i, part in enumerate(parts):
            place_keys(n, chunk, cycle_blocks, away[i * stacked : (i + 1) * stacked], part, keys)
    else:
        *parts, keys, packed = refs

    def finish(level, mask, value):
        current = digits[...]
        while level < LEVELS:
            change = switch(key_table(keys, level, cycle_blocks), current, cycle_blocks)
            mask = mask + change[0]
            value = value + automorph(value, level) + change[1]
            level += 1
            if level < LEVELS:
                current = toeplitz(automorph(mask, level))
        for p, words in enumerate((mask, value)):
            scaled = words.astype(jnp.float32) * 2.0**-32
            for b in range(cycle_blocks):
                packed[0, p : p + 1, b * LANES : (b + 1) * LANES] = scaled[b : b + 1, :]

    value = parts[0][:cycle_blocks, :]
    for part in parts[1:]:
        value = value + part[:cycle_blocks, :]
    if not chunk:
        finish(0, mask_in[...], value)
        return
    early = holds_first(n, stages)

    @pl.when(early)
    def _():
        finish(1, mask_in[...], value + automorph(value, 0) + change_in[...])

    @pl.when(jnp.logical_not(early))
    def _():
        finish(0, mask_in[...], value)


def near(x):
    return pltpu.with_memory_space_constraint(x, pltpu.VMEM)


def on_device(database, queries, key_rows, hint, assignment):
    n = lax.axis_size("col")
    polys, cycle_width = hint.shape
    clients = queries.shape[0]
    cycle_blocks = cycle_width // LANES
    key_width = key_rows.shape[1]
    stages = stages_of(n)
    vmem = pl.BlockSpec(memory_space=pltpu.VMEM)
    smem = pl.BlockSpec(memory_space=pltpu.SMEM)
    chunk = key_width // LANES if key_width % LANES == 0 else 0

    def exchange(x, mask):
        return lax.ppermute(x, "col", [(i, i ^ mask) for i in range(n)])

    pieces = len(stages[0]) + 1
    rows = n // pieces
    parts = pl.pallas_call(
        functools.partial(answer_kernel, n, polys),
        out_shape=[pltpu.VMEM((rows * (cycle_blocks + chunk), LANES), jnp.int32)] * pieces,
        in_specs=[smem, vmem, vmem, vmem],
        out_specs=[vmem] * pieces,
        scratch_shapes=[
            pltpu.VMEM((clients * polys * cycle_blocks, LANES), jnp.int32),
            pltpu.VMEM((max(clients * chunk, 8), LANES), jnp.int32),
        ],
    )(assignment, database, queries, key_rows)
    mask_poly, digits = pl.pallas_call(
        functools.partial(digit_kernel, polys),
        out_shape=[
            pltpu.VMEM((cycle_blocks, LANES), jnp.int32),
            pltpu.VMEM((2 * DIGITS * DEPTH, cycle_width), jnp.bfloat16),
        ],
        in_specs=[smem, vmem],
        out_specs=[vmem] * 2,
    )(assignment, hint)

    stacked = 1
    extra = []
    for step, stage in enumerate(stages):
        if chunk and step == len(stages) - 1:
            mask_poly, change, digits = pl.pallas_call(
                functools.partial(early_kernel, n, chunk),
                out_shape=[pltpu.VMEM(mask_poly.shape, jnp.int32)] * 2 + [pltpu.VMEM(digits.shape, jnp.bfloat16)],
                in_specs=[vmem] * 3,
                out_specs=[vmem] * 3,
                scratch_shapes=[pltpu.VMEM((n * chunk, LANES), jnp.int32)],
            )(near(mask_poly), near(digits), near(parts[0]))
            extra = [change]
        parts = [parts[0]] + [exchange(part, mask) for part, mask in zip(parts[1:], stage)]
        stacked *= len(parts)
        if step < len(stages) - 1:
            pieces = len(stages[step + 1]) + 1
            share = rows // pieces
            parts = pl.pallas_call(
                functools.partial(join_kernel, cycle_blocks, rows, chunk, len(parts)),
                out_shape=[pltpu.VMEM((share * (cycle_blocks + stacked * chunk), LANES), jnp.int32)] * pieces,
                in_specs=[vmem] * len(parts),
                out_specs=[vmem] * pieces,
            )(*map(near, parts))
            rows = share

    operands = [near(x) for x in (mask_poly, digits, *extra, *parts)]
    if not chunk:
        me = lax.axis_index("col")
        order = jnp.bitwise_xor(jnp.array(destinations(stages), jnp.int32), me)
        keys = jnp.take(key_rows, assignment[order] // polys, axis=0)[None]
        for stage in stages:
            cuts = jnp.split(keys, len(stage) + 1, axis=1)
            keys = jnp.concatenate([cuts[0]] + [exchange(x, mask) for x, mask in zip(cuts[1:], stage)], axis=0)
        away = sources(stages)
        places = jnp.array([away.index(i) for i in range(n)], jnp.int32)
        places = places[jnp.bitwise_xor(jnp.arange(n, dtype=jnp.int32), me)]
        operands.append(jnp.take(keys.reshape(n, key_width), places, axis=0).reshape(-1, LANES))
    return pl.pallas_call(
        functools.partial(pack_kernel, n, chunk, len(parts)),
        out_shape=jax.ShapeDtypeStruct((1, 2, cycle_width), jnp.float32),
        in_specs=[vmem] * len(operands),
        out_specs=vmem,
        scratch_shapes=[pltpu.VMEM((n * chunk, LANES), jnp.int32)] if chunk else [],
    )(*operands)


def solution(mesh):
    placed = (P("col", "grp"), P("grp", "col"), P("grp", "col"), P("grp", None), P("grp"))
    return jax.shard_map(
        on_device,
        mesh=mesh,
        in_specs=placed,
        out_specs=P(("grp", "col"), None, None),
        check_vma=False,
    )
```

```python
import functools

import jax
import jax.numpy as jnp
from jax import lax
from jax.experimental import pallas as pl
from jax.experimental.pallas import tpu as pltpu
from jax.sharding import PartitionSpec as P

LEVELS = 2
DIGITS = 2
LANES = 128
LOADS = 4
DEPTH = 64


def stages_of(n):
    bits = [1 << k for k in range(n.bit_length() - 1)]
    pair = [bits[1] | bits[2] | 1, bits[2] | 1, bits[1] | 1] if len(bits) > 2 else [b | 1 for b in bits[1:2]]
    return [[1]] + [pair] * (len(pair) > 0) + [[b | 1] for b in bits[3:]]


def destinations(stages):
    rows = [0]
    for stage in reversed(stages):
        rows = [r ^ mask for mask in [0] + stage for r in rows]
    return rows


def sources(stages):
    return destinations(stages[::-1])


def answer_kernel(n, polys, assignment, *refs):
    database, (queries, key_rows), refs = refs[:LOADS], refs[LOADS : LOADS + 2], refs[LOADS + 2 :]
    outs, (rows, key_scratch) = refs[:-2], refs[-2:]
    clients = queries.shape[0]
    blocks = LOADS * database[0].shape[1] // LANES
    cycle_blocks = blocks // polys
    words = queries[...]
    bytes_ = [jnp.bitwise_and(jnp.right_shift(words, 8 * j), 255) for j in range(4)]
    lhs = jnp.concatenate(bytes_, axis=0).astype(jnp.float32).astype(jnp.bfloat16)
    rhs = jnp.concatenate([part[...] for part in database], axis=1).astype(jnp.float32).astype(jnp.bfloat16)
    sums = jnp.dot(lhs, rhs, preferred_element_type=jnp.float32).astype(jnp.int32)
    partial = sums[:clients]
    for j in range(1, 4):
        partial = partial + jnp.left_shift(sums[j * clients : (j + 1) * clients], 8 * j)
    for m in range(blocks):
        rows[pl.ds(m, clients, stride=blocks), :] = partial[:, m * LANES : (m + 1) * LANES]
    share = n // len(outs)
    chunk = outs[0].shape[0] // share - cycle_blocks
    for m in range(chunk):
        key_scratch[pl.ds(m, clients, stride=chunk), :] = key_rows[:, m * LANES : (m + 1) * LANES]
    me = lax.axis_index("col")
    for r, mask in enumerate(destinations(stages_of(n))):
        unit = assignment[jnp.bitwise_xor(me, mask)]
        out, place = outs[r // share], r % share
        out[place * cycle_blocks : (place + 1) * cycle_blocks, :] = rows[
            pl.ds(pl.multiple_of(unit * cycle_blocks, cycle_blocks), cycle_blocks), :
        ]
        if chunk:
            first = share * cycle_blocks + place * chunk
            out[first : first + chunk, :] = key_scratch[pl.ds(unit // polys * chunk, chunk), :]


def join_kernel(cycle_blocks, rows, chunk, partners, *refs):
    parts, outs = refs[:partners], refs[partners:]
    share = rows // len(outs)
    cut = rows * cycle_blocks
    size = share * chunk
    for o, out in enumerate(outs):
        span = slice(o * share * cycle_blocks, (o + 1) * share * cycle_blocks)
        total = parts[0][span, :]
        for part in parts[1:]:
            total = total + part[span, :]
        out[: share * cycle_blocks, :] = total
        if chunk:
            stacked = (parts[0].shape[0] - cut) // (rows * chunk)
            for s in range(stacked * partners):
                source = cut + (s % stacked) * rows * chunk + o * size
                target = share * cycle_blocks + s * size
                out[target : target + size, :] = parts[s // stacked][source : source + size, :]


def shift_blocks(poly, count):
    blocks = poly.shape[0]
    whole, part = divmod(count % (2 * blocks), blocks)
    if part:
        row = lax.broadcasted_iota(jnp.int32, poly.shape, 0)
        poly = pltpu.roll(poly, part, 0)
        poly = jnp.where(row < part, -poly, poly)
    return -poly if whole else poly


def automorph(poly, level):
    blocks, lanes = poly.shape
    lane = lax.broadcasted_iota(jnp.int32, poly.shape, 1)
    period = 2 ** (level + 1)
    residue = jnp.bitwise_and(lane, period - 1)
    result = poly
    for m in range(1, period):
        result = jnp.where(residue == m, shift_blocks(poly, m * blocks // 2**level), result)
    return result


def toeplitz(word):
    blocks = word.shape[0]
    row = lax.broadcasted_iota(jnp.int32, (DEPTH, LANES), 0)
    lane = lax.broadcasted_iota(jnp.int32, (DEPTH, LANES), 1)
    inside = lane >= row
    turned = [
        pltpu.roll(jnp.broadcast_to(word[b : b + 1, :], (DEPTH, LANES)), 0, 1, stride=1, stride_axis=0)
        for b in range(blocks)
    ]
    columns = []
    for b in range(blocks):
        words = jnp.where(inside, turned[b], turned[b - 1])
        parts = []
        for j in range(4):
            part = jnp.bitwise_and(jnp.right_shift(words, 8 * j), 255).astype(jnp.float32)
            if b == 0:
                part = jnp.where(inside, part, -part)
            parts.append(part.astype(jnp.bfloat16))
        columns.append(jnp.concatenate(parts, axis=0))
    return jnp.concatenate(columns, axis=1)


def key_matrix(keys):
    lane = lax.broadcasted_iota(jnp.int32, keys[0][0].shape, 1)
    low = lane < DEPTH
    halves = [[None] * DIGITS for _ in range(4)]
    for p in range(2):
        for t in range(DIGITS):
            word = keys[t][p]
            other = pltpu.roll(word, DEPTH, 1)
            halves[2 * p][t] = jnp.where(low, word, jnp.left_shift(other, 8))
            halves[2 * p + 1][t] = jnp.where(low, other, jnp.left_shift(word, 8))
    rows = []
    for p in range(2):
        for s in range(4):
            for h in range(2):
                cut = [jnp.bitwise_and(jnp.right_shift(halves[2 * p + h][t], 8 * s), 255) for t in range(DIGITS)]
                rows.append(jnp.concatenate(cut, axis=1))
    return jnp.concatenate(rows, axis=0).astype(jnp.float32).astype(jnp.bfloat16)


def switch(keys, digits, blocks):
    sums = jnp.dot(key_matrix(keys), digits, preferred_element_type=jnp.float32).astype(jnp.int32)
    lane = lax.broadcasted_iota(jnp.int32, (blocks, LANES), 1)
    results = []
    for p in range(2):
        halves = []
        for h in range(2):
            total = None
            for m in range(blocks):
                joined = None
                for s in range(4):
                    first = ((p * 4 + s) * 2 + h) * blocks
                    piece = jnp.left_shift(sums[first : first + blocks, m * LANES : (m + 1) * LANES], 8 * s)
                    joined = piece if joined is None else joined + piece
                moved = shift_blocks(joined, m)
                total = moved if total is None else total + moved
            halves.append(total)
        turned = pltpu.roll(halves[1], DEPTH, 1)
        results.append(halves[0] + jnp.where(lane < DEPTH, shift_blocks(turned, 1), turned))
    return results


def digit_kernel(polys, assignment, hint, mask_out, digits_out):
    cycle_blocks = mask_out.shape[0]
    poly = assignment[lax.axis_index("col")] % polys
    row = hint[pl.ds(poly, 1), :]
    mask = jnp.concatenate([row[:, b * LANES : (b + 1) * LANES] for b in range(cycle_blocks)], axis=0)
    mask_out[...] = mask
    digits_out[...] = toeplitz(automorph(mask, 0))


def holds_first(n, stages):
    return jnp.logical_and(lax.axis_index("col") < n // 2, stages[-1] == [n // 2 + 1])


def key_table(keys, level, cycle_blocks):
    return [
        [keys[pl.ds(((level * DIGITS + t) * 2 + p) * cycle_blocks, cycle_blocks), :] for p in range(2)]
        for t in range(DIGITS)
    ]


def place_keys(n, chunk, cycle_blocks, away, part, keys):
    me = lax.axis_index("col")
    for slot, distance in enumerate(away):
        first = cycle_blocks + slot * chunk
        keys[pl.ds(jnp.bitwise_xor(me, distance) * chunk, chunk), :] = part[first : first + chunk, :]


def early_kernel(n, chunk, mask_in, digits_in, part, mask_out, change_out, digits_out, keys):
    stages = stages_of(n)
    early = holds_first(n, stages)
    cycle_blocks = mask_in.shape[0]

    @pl.when(early)
    def _():
        place_keys(n, chunk, cycle_blocks, sources(stages[:-1]), part, keys)
        change = switch(key_table(keys, 0, cycle_blocks), digits_in[...], cycle_blocks)
        mask = mask_in[...] + change[0]
        mask_out[...] = mask
        change_out[...] = change[1]
        digits_out[...] = toeplitz(automorph(mask, 1))

    @pl.when(jnp.logical_not(early))
    def _():
        mask_out[...] = mask_in[...]
        change_out[...] = jnp.zeros_like(change_out)
        digits_out[...] = digits_in[...]


def pack_kernel(n, chunk, partners, mask_in, digits, *refs):
    cycle_blocks = mask_in.shape[0]
    stages = stages_of(n)
    if chunk:
        change_in, *parts, packed, keys = refs
        stacked = n // partners
        away = sources(stages)
        for i, part in enumerate(parts):
            place_keys(n, chunk, cycle_blocks, away[i * stacked : (i + 1) * stacked], part, keys)
    else:
        *parts, keys, packed = refs

    def finish(level, mask, value):
        current = digits[...]
        while level < LEVELS:
            change = switch(key_table(keys, level, cycle_blocks), current, cycle_blocks)
            mask = mask + change[0]
            value = value + automorph(value, level) + change[1]
            level += 1
            if level < LEVELS:
                current = toeplitz(automorph(mask, level))
        for p, words in enumerate((mask, value)):
            scaled = words.astype(jnp.float32) * 2.0**-32
            for b in range(cycle_blocks):
                packed[0, p : p + 1, b * LANES : (b + 1) * LANES] = scaled[b : b + 1, :]

    value = parts[0][:cycle_blocks, :]
    for part in parts[1:]:
        value = value + part[:cycle_blocks, :]
    if not chunk:
        finish(0, mask_in[...], value)
        return
    early = holds_first(n, stages)

    @pl.when(early)
    def _():
        finish(1, mask_in[...], value + automorph(value, 0) + change_in[...])

    @pl.when(jnp.logical_not(early))
    def _():
        finish(0, mask_in[...], value)


def near(x):
    return pltpu.with_memory_space_constraint(x, pltpu.VMEM)


def on_device(database, queries, key_rows, hint, assignment):
    n = lax.axis_size("col")
    polys, cycle_width = hint.shape
    clients = queries.shape[0]
    cycle_blocks = cycle_width // LANES
    key_width = key_rows.shape[1]
    stages = stages_of(n)
    vmem = pl.BlockSpec(memory_space=pltpu.VMEM)
    smem = pl.BlockSpec(memory_space=pltpu.SMEM)
    chunk = key_width // LANES if key_width % LANES == 0 else 0

    def exchange(x, mask):
        return lax.ppermute(x, "col", [(i, i ^ mask) for i in range(n)])

    width = database.shape[1] // LOADS
    columns = [pl.BlockSpec((database.shape[0], width), lambda _, i=i: (0, i)) for i in range(LOADS)]
    pieces = len(stages[0]) + 1
    rows = n // pieces
    parts = pl.pallas_call(
        functools.partial(answer_kernel, n, polys),
        out_shape=[pltpu.VMEM((rows * (cycle_blocks + chunk), LANES), jnp.int32)] * pieces,
        grid=(1,),
        in_specs=[smem, *columns, vmem, vmem],
        out_specs=[vmem] * pieces,
        scratch_shapes=[
            pltpu.VMEM((clients * polys * cycle_blocks, LANES), jnp.int32),
            pltpu.VMEM((max(clients * chunk, 8), LANES), jnp.int32),
        ],
    )(assignment, *[database] * LOADS, queries, key_rows)
    mask_poly, digits = pl.pallas_call(
        functools.partial(digit_kernel, polys),
        out_shape=[
            pltpu.VMEM((cycle_blocks, LANES), jnp.int32),
            pltpu.VMEM((2 * DIGITS * DEPTH, cycle_width), jnp.bfloat16),
        ],
        in_specs=[smem, vmem],
        out_specs=[vmem] * 2,
    )(assignment, hint)

    stacked = 1
    extra = []
    for step, stage in enumerate(stages):
        if chunk and step == len(stages) - 1:
            mask_poly, change, digits = pl.pallas_call(
                functools.partial(early_kernel, n, chunk),
                out_shape=[pltpu.VMEM(mask_poly.shape, jnp.int32)] * 2 + [pltpu.VMEM(digits.shape, jnp.bfloat16)],
                in_specs=[vmem] * 3,
                out_specs=[vmem] * 3,
                scratch_shapes=[pltpu.VMEM((n * chunk, LANES), jnp.int32)],
            )(near(mask_poly), near(digits), near(parts[0]))
            extra = [change]
        parts = [parts[0]] + [exchange(part, mask) for part, mask in zip(parts[1:], stage)]
        stacked *= len(parts)
        if step < len(stages) - 1:
            pieces = len(stages[step + 1]) + 1
            share = rows // pieces
            parts = pl.pallas_call(
                functools.partial(join_kernel, cycle_blocks, rows, chunk, len(parts)),
                out_shape=[pltpu.VMEM((share * (cycle_blocks + stacked * chunk), LANES), jnp.int32)] * pieces,
                in_specs=[vmem] * len(parts),
                out_specs=[vmem] * pieces,
            )(*map(near, parts))
            rows = share

    operands = [near(x) for x in (mask_poly, digits, *extra, *parts)]
    if not chunk:
        me = lax.axis_index("col")
        order = jnp.bitwise_xor(jnp.array(destinations(stages), jnp.int32), me)
        keys = jnp.take(key_rows, assignment[order] // polys, axis=0)[None]
        for stage in stages:
            cuts = jnp.split(keys, len(stage) + 1, axis=1)
            keys = jnp.concatenate([cuts[0]] + [exchange(x, mask) for x, mask in zip(cuts[1:], stage)], axis=0)
        away = sources(stages)
        places = jnp.array([away.index(i) for i in range(n)], jnp.int32)
        places = places[jnp.bitwise_xor(jnp.arange(n, dtype=jnp.int32), me)]
        operands.append(jnp.take(keys.reshape(n, key_width), places, axis=0).reshape(-1, LANES))
    return pl.pallas_call(
        functools.partial(pack_kernel, n, chunk, len(parts)),
        out_shape=jax.ShapeDtypeStruct((1, 2, cycle_width), jnp.float32),
        in_specs=[vmem] * len(operands),
        out_specs=vmem,
        scratch_shapes=[pltpu.VMEM((n * chunk, LANES), jnp.int32)] if chunk else [],
    )(*operands)


def solution(mesh):
    placed = (P("col", "grp"), P("grp", "col"), P("grp", "col"), P("grp", None), P("grp"))
    return jax.shard_map(
        on_device,
        mesh=mesh,
        in_specs=placed,
        out_specs=P(("grp", "col"), None, None),
        check_vma=False,
    )
```

```python
import functools

import jax
import jax.numpy as jnp
from jax import lax
from jax.experimental import pallas as pl
from jax.experimental.pallas import tpu as pltpu
from jax.sharding import PartitionSpec as P

LEVELS = 2
DIGITS = 2
LANES = 128
LOADS = 4
DEPTH = 64


def stages_of(n):
    bits = [1 << k for k in range(n.bit_length() - 1)]
    pair = [(3, 1), (7, 1), (5, 0)] if len(bits) > 2 else [(b | 1, 0) for b in bits[1:2]]
    return [[(1, 0)]] + [pair] * (len(pair) > 0) + [[(b | 1, 0)] for b in bits[3:]]


def moved(move, i):
    mask, twist = move
    if twist:
        return i ^ mask ^ ((i & 2) << 1)
    return i ^ mask


def back(move):
    mask, twist = move
    return (mask ^ (mask & 2) << 1 if twist else mask, twist)


def follow(steps, i):
    for move in steps:
        i = moved(move, i)
    return i


def destinations(stages, me):
    rows = [[]]
    for stage in reversed(stages):
        rows = rows + [[move] + row for move in stage for row in rows]
    return [follow(row, me) for row in rows]


def sources(stages, me):
    blocks = [[]]
    for stage in stages:
        blocks = blocks + [[back(move)] + block for move in stage for block in blocks]
    return [follow(block, me) for block in blocks]


def answer_kernel(n, polys, assignment, *refs):
    database, (queries, key_rows), refs = refs[:LOADS], refs[LOADS : LOADS + 2], refs[LOADS + 2 :]
    outs, (rows, key_scratch) = refs[:-2], refs[-2:]
    clients = queries.shape[0]
    blocks = LOADS * database[0].shape[1] // LANES
    cycle_blocks = blocks // polys
    words = queries[...]
    bytes_ = [jnp.bitwise_and(jnp.right_shift(words, 8 * j), 255) for j in range(4)]
    lhs = jnp.concatenate(bytes_, axis=0).astype(jnp.float32).astype(jnp.bfloat16)
    rhs = jnp.concatenate([part[...] for part in database], axis=1).astype(jnp.float32).astype(jnp.bfloat16)
    sums = jnp.dot(lhs, rhs, preferred_element_type=jnp.float32).astype(jnp.int32)
    partial = sums[:clients]
    for j in range(1, 4):
        partial = partial + jnp.left_shift(sums[j * clients : (j + 1) * clients], 8 * j)
    for m in range(blocks):
        rows[pl.ds(m, clients, stride=blocks), :] = partial[:, m * LANES : (m + 1) * LANES]
    share = n // len(outs)
    chunk = outs[0].shape[0] // share - cycle_blocks
    for m in range(chunk):
        key_scratch[pl.ds(m, clients, stride=chunk), :] = key_rows[:, m * LANES : (m + 1) * LANES]
    me = lax.axis_index("col")
    for r, owner in enumerate(destinations(stages_of(n), me)):
        unit = assignment[owner]
        out, place = outs[r // share], r % share
        out[place * cycle_blocks : (place + 1) * cycle_blocks, :] = rows[
            pl.ds(pl.multiple_of(unit * cycle_blocks, cycle_blocks), cycle_blocks), :
        ]
        if chunk:
            first = share * cycle_blocks + place * chunk
            out[first : first + chunk, :] = key_scratch[pl.ds(unit // polys * chunk, chunk), :]


def join_kernel(cycle_blocks, rows, chunk, partners, *refs):
    parts, outs = refs[:partners], refs[partners:]
    share = rows // len(outs)
    cut = rows * cycle_blocks
    size = share * chunk
    for o, out in enumerate(outs):
        span = slice(o * share * cycle_blocks, (o + 1) * share * cycle_blocks)
        total = parts[0][span, :]
        for part in parts[1:]:
            total = total + part[span, :]
        out[: share * cycle_blocks, :] = total
        if chunk:
            stacked = (parts[0].shape[0] - cut) // (rows * chunk)
            for s in range(stacked * partners):
                source = cut + (s % stacked) * rows * chunk + o * size
                target = share * cycle_blocks + s * size
                out[target : target + size, :] = parts[s // stacked][source : source + size, :]


def shift_blocks(poly, count):
    blocks = poly.shape[0]
    whole, part = divmod(count % (2 * blocks), blocks)
    if part:
        row = lax.broadcasted_iota(jnp.int32, poly.shape, 0)
        poly = pltpu.roll(poly, part, 0)
        poly = jnp.where(row < part, -poly, poly)
    return -poly if whole else poly


def automorph(poly, level):
    blocks, lanes = poly.shape
    lane = lax.broadcasted_iota(jnp.int32, poly.shape, 1)
    period = 2 ** (level + 1)
    residue = jnp.bitwise_and(lane, period - 1)
    result = poly
    for m in range(1, period):
        result = jnp.where(residue == m, shift_blocks(poly, m * blocks // 2**level), result)
    return result


def toeplitz(word):
    blocks = word.shape[0]
    row = lax.broadcasted_iota(jnp.int32, (DEPTH, LANES), 0)
    lane = lax.broadcasted_iota(jnp.int32, (DEPTH, LANES), 1)
    inside = lane >= row
    turned = [
        pltpu.roll(jnp.broadcast_to(word[b : b + 1, :], (DEPTH, LANES)), 0, 1, stride=1, stride_axis=0)
        for b in range(blocks)
    ]
    columns = []
    for b in range(blocks):
        words = jnp.where(inside, turned[b], turned[b - 1])
        parts = []
        for j in range(4):
            part = jnp.bitwise_and(jnp.right_shift(words, 8 * j), 255).astype(jnp.float32)
            if b == 0:
                part = jnp.where(inside, part, -part)
            parts.append(part.astype(jnp.bfloat16))
        columns.append(jnp.concatenate(parts, axis=0))
    return jnp.concatenate(columns, axis=1)


def key_matrix(keys):
    lane = lax.broadcasted_iota(jnp.int32, keys[0][0].shape, 1)
    low = lane < DEPTH
    halves = [[None] * DIGITS for _ in range(4)]
    for p in range(2):
        for t in range(DIGITS):
            word = keys[t][p]
            other = pltpu.roll(word, DEPTH, 1)
            halves[2 * p][t] = jnp.where(low, word, jnp.left_shift(other, 8))
            halves[2 * p + 1][t] = jnp.where(low, other, jnp.left_shift(word, 8))
    rows = []
    for p in range(2):
        for s in range(4):
            for h in range(2):
                cut = [jnp.bitwise_and(jnp.right_shift(halves[2 * p + h][t], 8 * s), 255) for t in range(DIGITS)]
                rows.append(jnp.concatenate(cut, axis=1))
    return jnp.concatenate(rows, axis=0).astype(jnp.float32).astype(jnp.bfloat16)


def switch(matrix, digits, blocks):
    sums = jnp.dot(matrix, digits, preferred_element_type=jnp.float32).astype(jnp.int32)
    lane = lax.broadcasted_iota(jnp.int32, (blocks, LANES), 1)
    results = []
    for p in range(2):
        halves = []
        for h in range(2):
            total = None
            for m in range(blocks):
                joined = None
                for s in range(4):
                    first = ((p * 4 + s) * 2 + h) * blocks
                    piece = jnp.left_shift(sums[first : first + blocks, m * LANES : (m + 1) * LANES], 8 * s)
                    joined = piece if joined is None else joined + piece
                moved = shift_blocks(joined, m)
                total = moved if total is None else total + moved
            halves.append(total)
        turned = pltpu.roll(halves[1], DEPTH, 1)
        results.append(halves[0] + jnp.where(lane < DEPTH, shift_blocks(turned, 1), turned))
    return results


def digit_kernel(polys, assignment, hint, mask_out, digits_out):
    cycle_blocks = mask_out.shape[0]
    poly = assignment[lax.axis_index("col")] % polys
    row = hint[pl.ds(poly, 1), :]
    mask = jnp.concatenate([row[:, b * LANES : (b + 1) * LANES] for b in range(cycle_blocks)], axis=0)
    mask_out[...] = mask
    digits_out[...] = toeplitz(automorph(mask, 0))


def halves_by_level(n, stages):
    return LEVELS == 2 and stages[-1] == [(n // 2 + 1, 0)]


def level_matrix(keys, level, cycle_blocks):
    table = [
        [keys[pl.ds(((level * DIGITS + t) * 2 + p) * cycle_blocks, cycle_blocks), :] for p in range(2)]
        for t in range(DIGITS)
    ]
    return key_matrix(table)


def place_keys(total, chunk, cycle_blocks, origins, part, keys):
    for slot, origin in enumerate(origins):
        first = cycle_blocks + slot * chunk
        keys[pl.ds((origin & (total - 1)) * chunk, chunk), :] = part[first : first + chunk, :]


def early_kernel(n, chunk, mask_in, digits_in, part, mask_out, change_out, digits_out, matrix_out, keys):
    cycle_blocks = mask_in.shape[0]
    place_keys(n // 2, chunk, cycle_blocks, sources(stages_of(n)[:-1], lax.axis_index("col")), part, keys)
    matrix = level_matrix(keys, 0, cycle_blocks)
    matrix_out[...] = matrix
    early = lax.axis_index("col") < n // 2

    @pl.when(early)
    def _():
        change = switch(matrix, digits_in[...], cycle_blocks)
        mask = mask_in[...] + change[0]
        mask_out[...] = mask
        change_out[...] = change[1]
        digits_out[...] = toeplitz(automorph(mask, 1))

    @pl.when(jnp.logical_not(early))
    def _():
        mask_out[...] = mask_in[...]
        change_out[...] = jnp.zeros_like(change_out)
        digits_out[...] = digits_in[...]


def finish(level, mask, value, digits, matrices, packed):
    cycle_blocks = mask.shape[0]
    for i, matrix in enumerate(matrices):
        current = digits[...] if i == 0 else toeplitz(automorph(mask, level))
        change = switch(matrix(), current, cycle_blocks)
        mask = mask + change[0]
        value = value + automorph(value, level) + change[1]
        level += 1
    for p, words in enumerate((mask, value)):
        scaled = words.astype(jnp.float32) * 2.0**-32
        for b in range(cycle_blocks):
            packed[0, p : p + 1, b * LANES : (b + 1) * LANES] = scaled[b : b + 1, :]


def sum_answers(parts, cycle_blocks):
    value = parts[0][:cycle_blocks, :]
    for part in parts[1:]:
        value = value + part[:cycle_blocks, :]
    return value


def late_kernel(n, chunk, mask_in, digits, change_in, own_matrix, own, got, packed, keys):
    cycle_blocks = mask_in.shape[0]
    origins = sources(stages_of(n), lax.axis_index("col"))
    early = lax.axis_index("col") < n // 2

    def received():
        place_keys(n // 2, chunk, cycle_blocks, origins[n // 2 :], got, keys)
        return level_matrix(keys, 0, cycle_blocks)

    @pl.when(early)
    def _():
        value = sum_answers((own, got), cycle_blocks)
        finish(1, mask_in[...], value + automorph(value, 0) + change_in[...], digits, [received], packed)

    @pl.when(jnp.logical_not(early))
    def _():
        value = sum_answers((own, got), cycle_blocks)
        finish(0, mask_in[...], value, digits, [received, lambda: own_matrix[...]], packed)


def pack_kernel(n, chunk, partners, mask_in, digits, *refs):
    cycle_blocks = mask_in.shape[0]
    if chunk:
        *parts, packed, keys = refs
        stacked = n // partners
        away = sources(stages_of(n), lax.axis_index("col"))
        for i, part in enumerate(parts):
            place_keys(n, chunk, cycle_blocks, away[i * stacked : (i + 1) * stacked], part, keys)
    else:
        *parts, keys, packed = refs
    matrices = [functools.partial(level_matrix, keys, level, cycle_blocks) for level in range(LEVELS)]
    finish(0, mask_in[...], sum_answers(parts, cycle_blocks), digits, matrices, packed)


def near(x):
    return pltpu.with_memory_space_constraint(x, pltpu.VMEM)


def on_device(database, queries, key_rows, hint, assignment):
    n = lax.axis_size("col")
    polys, cycle_width = hint.shape
    clients = queries.shape[0]
    cycle_blocks = cycle_width // LANES
    key_width = key_rows.shape[1]
    stages = stages_of(n)
    vmem = pl.BlockSpec(memory_space=pltpu.VMEM)
    smem = pl.BlockSpec(memory_space=pltpu.SMEM)
    chunk = key_width // LANES if key_width % LANES == 0 else 0

    def exchange(x, move):
        return lax.ppermute(x, "col", [(i, moved(move, i)) for i in range(n)])

    width = database.shape[1] // LOADS
    columns = [pl.BlockSpec((database.shape[0], width), lambda _, i=i: (0, i)) for i in range(LOADS)]
    pieces = len(stages[0]) + 1
    rows = n // pieces
    parts = pl.pallas_call(
        functools.partial(answer_kernel, n, polys),
        out_shape=[pltpu.VMEM((rows * (cycle_blocks + chunk), LANES), jnp.int32)] * pieces,
        grid=(1,),
        in_specs=[smem, *columns, vmem, vmem],
        out_specs=[vmem] * pieces,
        scratch_shapes=[
            pltpu.VMEM((clients * polys * cycle_blocks, LANES), jnp.int32),
            pltpu.VMEM((max(clients * chunk, 8), LANES), jnp.int32),
        ],
    )(assignment, *[database] * LOADS, queries, key_rows)
    mask_poly, digits = pl.pallas_call(
        functools.partial(digit_kernel, polys),
        out_shape=[
            pltpu.VMEM((cycle_blocks, LANES), jnp.int32),
            pltpu.VMEM((2 * DIGITS * DEPTH, cycle_width), jnp.bfloat16),
        ],
        in_specs=[smem, vmem],
        out_specs=[vmem] * 2,
    )(assignment, hint)

    stacked = 1
    extra = []
    halves = chunk and halves_by_level(n, stages)
    for step, stage in enumerate(stages):
        if halves and step == len(stages) - 1:
            matrix = (2 * 4 * 2 * cycle_blocks, 2 * DIGITS * DEPTH)
            mask_poly, change, digits, own_matrix = pl.pallas_call(
                functools.partial(early_kernel, n, chunk),
                out_shape=[pltpu.VMEM(mask_poly.shape, jnp.int32)] * 2
                + [pltpu.VMEM(digits.shape, jnp.bfloat16), pltpu.VMEM(matrix, jnp.bfloat16)],
                in_specs=[vmem] * 3,
                out_specs=[vmem] * 4,
                scratch_shapes=[pltpu.VMEM((n // 2 * chunk, LANES), jnp.int32)],
            )(near(mask_poly), near(digits), near(parts[0]))
            extra = [change, own_matrix]
        parts = [parts[0]] + [exchange(part, move) for part, move in zip(parts[1:], stage)]
        stacked *= len(parts)
        if step < len(stages) - 1:
            pieces = len(stages[step + 1]) + 1
            share = rows // pieces
            parts = pl.pallas_call(
                functools.partial(join_kernel, cycle_blocks, rows, chunk, len(parts)),
                out_shape=[pltpu.VMEM((share * (cycle_blocks + stacked * chunk), LANES), jnp.int32)] * pieces,
                in_specs=[vmem] * len(parts),
                out_specs=[vmem] * pieces,
            )(*map(near, parts))
            rows = share

    operands = [near(x) for x in (mask_poly, digits, *extra, *parts)]
    if not chunk:
        me = lax.axis_index("col")
        owners = assignment[jnp.stack(destinations(stages, me))] // polys
        keys = jnp.take(key_rows, owners, axis=0)[None]
        for stage in stages:
            cuts = jnp.split(keys, len(stage) + 1, axis=1)
            keys = jnp.concatenate([cuts[0]] + [exchange(x, move) for x, move in zip(cuts[1:], stage)], axis=0)
        places = jnp.zeros((n,), jnp.int32).at[jnp.stack(sources(stages, me))].set(jnp.arange(n, dtype=jnp.int32))
        operands.append(jnp.take(keys.reshape(n, key_width), places, axis=0).reshape(-1, LANES))
    return pl.pallas_call(
        functools.partial(late_kernel, n, chunk) if halves else functools.partial(pack_kernel, n, chunk, len(parts)),
        out_shape=jax.ShapeDtypeStruct((1, 2, cycle_width), jnp.float32),
        in_specs=[vmem] * len(operands),
        out_specs=vmem,
        scratch_shapes=[pltpu.VMEM((n * chunk, LANES), jnp.int32)] if chunk else [],
    )(*operands)


def solution(mesh):
    placed = (P("col", "grp"), P("grp", "col"), P("grp", "col"), P("grp", None), P("grp"))
    return jax.shard_map(
        on_device,
        mesh=mesh,
        in_specs=placed,
        out_specs=P(("grp", "col"), None, None),
        check_vma=False,
    )
```

```python
import functools

import jax
import jax.numpy as jnp
from jax import lax
from jax.experimental import pallas as pl
from jax.experimental.pallas import tpu as pltpu
from jax.sharding import PartitionSpec as P

LEVELS = 2
DIGITS = 2
LANES = 128
LOADS = 4
DEPTH = 64


def stages_of(n):
    bits = [1 << k for k in range(n.bit_length() - 1)]
    pair = [(3, 1), (7, 1), (5, 0)] if len(bits) > 2 else [(b | 1, 0) for b in bits[1:2]]
    return [[(1, 0)]] + [pair] * (len(pair) > 0) + [[(b | 1, 0)] for b in bits[3:]]


def moved(move, i):
    mask, twist = move
    if twist:
        return i ^ mask ^ ((i & 2) << 1)
    return i ^ mask


def back(move):
    mask, twist = move
    return (mask ^ (mask & 2) << 1 if twist else mask, twist)


def follow(steps, i):
    for move in steps:
        i = moved(move, i)
    return i


def destinations(stages, me):
    rows = [[]]
    for stage in reversed(stages):
        rows = rows + [[move] + row for move in stage for row in rows]
    return [follow(row, me) for row in rows]


def sources(stages, me):
    blocks = [[]]
    for stage in stages:
        blocks = blocks + [[back(move)] + block for move in stage for block in blocks]
    return [follow(block, me) for block in blocks]


def answer_kernel(n, polys, assignment, *refs):
    database, (queries, key_rows), refs = refs[:LOADS], refs[LOADS : LOADS + 2], refs[LOADS + 2 :]
    outs, (rows, key_scratch) = refs[:-2], refs[-2:]
    clients = queries.shape[0]
    blocks = LOADS * database[0].shape[1] // LANES
    cycle_blocks = blocks // polys
    words = queries[...]
    bytes_ = [jnp.bitwise_and(jnp.right_shift(words, 8 * j), 255) for j in range(4)]
    lhs = jnp.concatenate(bytes_, axis=0).astype(jnp.float32).astype(jnp.bfloat16)
    rhs = jnp.concatenate([part[...] for part in database], axis=1).astype(jnp.float32).astype(jnp.bfloat16)
    sums = jnp.dot(lhs, rhs, preferred_element_type=jnp.float32).astype(jnp.int32)
    partial = sums[:clients]
    for j in range(1, 4):
        partial = partial + jnp.left_shift(sums[j * clients : (j + 1) * clients], 8 * j)
    for m in range(blocks):
        rows[pl.ds(m, clients, stride=blocks), :] = partial[:, m * LANES : (m + 1) * LANES]
    share = n // len(outs)
    chunk = outs[0].shape[0] // share - cycle_blocks
    for m in range(chunk):
        key_scratch[pl.ds(m, clients, stride=chunk), :] = key_rows[:, m * LANES : (m + 1) * LANES]
    me = lax.axis_index("col")
    for r, owner in enumerate(destinations(stages_of(n), me)):
        unit = assignment[owner]
        out, place = outs[r // share], r % share
        out[place * cycle_blocks : (place + 1) * cycle_blocks, :] = rows[
            pl.ds(pl.multiple_of(unit * cycle_blocks, cycle_blocks), cycle_blocks), :
        ]
        if chunk:
            first = share * cycle_blocks + place * chunk
            out[first : first + chunk, :] = key_scratch[pl.ds(unit // polys * chunk, chunk), :]


def join_kernel(cycle_blocks, rows, chunk, partners, after, *refs):
    del after
    parts, outs = refs[:partners], refs[partners:]
    share = rows // len(outs)
    cut = rows * cycle_blocks
    size = share * chunk
    for o, out in enumerate(outs):
        span = slice(o * share * cycle_blocks, (o + 1) * share * cycle_blocks)
        total = parts[0][span, :]
        for part in parts[1:]:
            total = total + part[span, :]
        out[: share * cycle_blocks, :] = total
        if chunk:
            stacked = (parts[0].shape[0] - cut) // (rows * chunk)
            for s in range(stacked * partners):
                source = cut + (s % stacked) * rows * chunk + o * size
                target = share * cycle_blocks + s * size
                out[target : target + size, :] = parts[s // stacked][source : source + size, :]


def shift_blocks(poly, count):
    blocks = poly.shape[0]
    whole, part = divmod(count % (2 * blocks), blocks)
    if part:
        row = lax.broadcasted_iota(jnp.int32, poly.shape, 0)
        poly = pltpu.roll(poly, part, 0)
        poly = jnp.where(row < part, -poly, poly)
    return -poly if whole else poly


def automorph(poly, level):
    blocks, lanes = poly.shape
    lane = lax.broadcasted_iota(jnp.int32, poly.shape, 1)
    period = 2 ** (level + 1)
    residue = jnp.bitwise_and(lane, period - 1)
    result = poly
    for m in range(1, period):
        result = jnp.where(residue == m, shift_blocks(poly, m * blocks // 2**level), result)
    return result


def toeplitz(word):
    blocks = word.shape[0]
    row = lax.broadcasted_iota(jnp.int32, (DEPTH, LANES), 0)
    lane = lax.broadcasted_iota(jnp.int32, (DEPTH, LANES), 1)
    inside = lane >= row
    turned = [
        pltpu.roll(jnp.broadcast_to(word[b : b + 1, :], (DEPTH, LANES)), 0, 1, stride=1, stride_axis=0)
        for b in range(blocks)
    ]
    columns = []
    for b in range(blocks):
        words = jnp.where(inside, turned[b], turned[b - 1])
        parts = []
        for j in range(4):
            part = jnp.bitwise_and(jnp.right_shift(words, 8 * j), 255).astype(jnp.float32)
            if b == 0:
                part = jnp.where(inside, part, -part)
            parts.append(part.astype(jnp.bfloat16))
        columns.append(jnp.concatenate(parts, axis=0))
    return jnp.concatenate(columns, axis=1)


def key_matrix(keys):
    lane = lax.broadcasted_iota(jnp.int32, keys[0][0].shape, 1)
    low = lane < DEPTH
    halves = [[None] * DIGITS for _ in range(4)]
    for p in range(2):
        for t in range(DIGITS):
            word = keys[t][p]
            other = pltpu.roll(word, DEPTH, 1)
            halves[2 * p][t] = jnp.where(low, word, jnp.left_shift(other, 8))
            halves[2 * p + 1][t] = jnp.where(low, other, jnp.left_shift(word, 8))
    rows = []
    for p in range(2):
        for s in range(4):
            for h in range(2):
                cut = [jnp.bitwise_and(jnp.right_shift(halves[2 * p + h][t], 8 * s), 255) for t in range(DIGITS)]
                rows.append(jnp.concatenate(cut, axis=1))
    return jnp.concatenate(rows, axis=0).astype(jnp.float32).astype(jnp.bfloat16)


def switch(matrix, digits, blocks):
    sums = jnp.dot(matrix, digits, preferred_element_type=jnp.float32).astype(jnp.int32)
    lane = lax.broadcasted_iota(jnp.int32, (blocks, LANES), 1)
    results = []
    for p in range(2):
        halves = []
        for h in range(2):
            total = None
            for m in range(blocks):
                joined = None
                for s in range(4):
                    first = ((p * 4 + s) * 2 + h) * blocks
                    piece = jnp.left_shift(sums[first : first + blocks, m * LANES : (m + 1) * LANES], 8 * s)
                    joined = piece if joined is None else joined + piece
                moved = shift_blocks(joined, m)
                total = moved if total is None else total + moved
            halves.append(total)
        turned = pltpu.roll(halves[1], DEPTH, 1)
        results.append(halves[0] + jnp.where(lane < DEPTH, shift_blocks(turned, 1), turned))
    return results


def digit_kernel(polys, assignment, hint, after, mask_out, digits_out):
    del after
    cycle_blocks = mask_out.shape[0]
    poly = assignment[lax.axis_index("col")] % polys
    row = hint[pl.ds(poly, 1), :]
    mask = jnp.concatenate([row[:, b * LANES : (b + 1) * LANES] for b in range(cycle_blocks)], axis=0)
    mask_out[...] = mask
    digits_out[...] = toeplitz(automorph(mask, 0))


def halves_by_level(n, stages):
    return LEVELS == 2 and stages[-1] == [(n // 2 + 1, 0)]


def level_matrix(keys, level, cycle_blocks):
    table = [
        [keys[pl.ds(((level * DIGITS + t) * 2 + p) * cycle_blocks, cycle_blocks), :] for p in range(2)]
        for t in range(DIGITS)
    ]
    return key_matrix(table)


def place_keys(total, chunk, cycle_blocks, origins, part, keys):
    for slot, origin in enumerate(origins):
        first = cycle_blocks + slot * chunk
        keys[pl.ds((origin & (total - 1)) * chunk, chunk), :] = part[first : first + chunk, :]


def early_kernel(n, chunk, mask_in, digits_in, part, mask_out, change_out, digits_out, matrix_out, keys):
    cycle_blocks = mask_in.shape[0]
    place_keys(n // 2, chunk, cycle_blocks, sources(stages_of(n)[:-1], lax.axis_index("col")), part, keys)
    matrix = level_matrix(keys, 0, cycle_blocks)
    matrix_out[...] = matrix
    early = lax.axis_index("col") < n // 2

    @pl.when(early)
    def _():
        change = switch(matrix, digits_in[...], cycle_blocks)
        mask = mask_in[...] + change[0]
        mask_out[...] = mask
        change_out[...] = change[1]
        digits_out[...] = toeplitz(automorph(mask, 1))

    @pl.when(jnp.logical_not(early))
    def _():
        mask_out[...] = mask_in[...]
        change_out[...] = jnp.zeros_like(change_out)
        digits_out[...] = digits_in[...]


def finish(level, mask, value, digits, matrices, packed):
    cycle_blocks = mask.shape[0]
    for i, matrix in enumerate(matrices):
        current = digits[...] if i == 0 else toeplitz(automorph(mask, level))
        change = switch(matrix(), current, cycle_blocks)
        mask = mask + change[0]
        value = value + automorph(value, level) + change[1]
        level += 1
    for p, words in enumerate((mask, value)):
        scaled = words.astype(jnp.float32) * 2.0**-32
        for b in range(cycle_blocks):
            packed[0, p : p + 1, b * LANES : (b + 1) * LANES] = scaled[b : b + 1, :]


def sum_answers(parts, cycle_blocks):
    value = parts[0][:cycle_blocks, :]
    for part in parts[1:]:
        value = value + part[:cycle_blocks, :]
    return value


def late_kernel(n, chunk, mask_in, digits, change_in, own_matrix, own, got, packed, keys):
    cycle_blocks = mask_in.shape[0]
    origins = sources(stages_of(n), lax.axis_index("col"))
    early = lax.axis_index("col") < n // 2

    def received():
        place_keys(n // 2, chunk, cycle_blocks, origins[n // 2 :], got, keys)
        return level_matrix(keys, 0, cycle_blocks)

    @pl.when(early)
    def _():
        value = sum_answers((own, got), cycle_blocks)
        finish(1, mask_in[...], value + automorph(value, 0) + change_in[...], digits, [received], packed)

    @pl.when(jnp.logical_not(early))
    def _():
        value = sum_answers((own, got), cycle_blocks)
        finish(0, mask_in[...], value, digits, [received, lambda: own_matrix[...]], packed)


def pack_kernel(n, chunk, partners, mask_in, digits, *refs):
    cycle_blocks = mask_in.shape[0]
    if chunk:
        *parts, packed, keys = refs
        stacked = n // partners
        away = sources(stages_of(n), lax.axis_index("col"))
        for i, part in enumerate(parts):
            place_keys(n, chunk, cycle_blocks, away[i * stacked : (i + 1) * stacked], part, keys)
    else:
        *parts, keys, packed = refs
    matrices = [functools.partial(level_matrix, keys, level, cycle_blocks) for level in range(LEVELS)]
    finish(0, mask_in[...], sum_answers(parts, cycle_blocks), digits, matrices, packed)


def near(x):
    return pltpu.with_memory_space_constraint(x, pltpu.VMEM)


def on_device(database, queries, key_rows, hint, assignment):
    n = lax.axis_size("col")
    polys, cycle_width = hint.shape
    clients = queries.shape[0]
    cycle_blocks = cycle_width // LANES
    key_width = key_rows.shape[1]
    stages = stages_of(n)
    vmem = pl.BlockSpec(memory_space=pltpu.VMEM)
    smem = pl.BlockSpec(memory_space=pltpu.SMEM)
    anywhere = pl.BlockSpec(memory_space=pl.ANY)
    chunk = key_width // LANES if key_width % LANES == 0 else 0

    def exchange(x, move):
        return lax.ppermute(x, "col", [(i, moved(move, i)) for i in range(n)])

    width = database.shape[1] // LOADS
    columns = [pl.BlockSpec((database.shape[0], width), lambda _, i=i: (0, i)) for i in range(LOADS)]
    pieces = len(stages[0]) + 1
    rows = n // pieces
    parts = pl.pallas_call(
        functools.partial(answer_kernel, n, polys),
        out_shape=[pltpu.VMEM((rows * (cycle_blocks + chunk), LANES), jnp.int32)] * pieces,
        grid=(1,),
        in_specs=[smem, *columns, vmem, vmem],
        out_specs=[vmem] * pieces,
        scratch_shapes=[
            pltpu.VMEM((clients * polys * cycle_blocks, LANES), jnp.int32),
            pltpu.VMEM((max(clients * chunk, 8), LANES), jnp.int32),
        ],
    )(assignment, *[database] * LOADS, queries, key_rows)
    def digits_after(after):
        return pl.pallas_call(
            functools.partial(digit_kernel, polys),
            out_shape=[
                pltpu.VMEM((cycle_blocks, LANES), jnp.int32),
                pltpu.VMEM((2 * DIGITS * DEPTH, cycle_width), jnp.bfloat16),
            ],
            in_specs=[smem, vmem, anywhere],
            out_specs=[vmem] * 2,
        )(assignment, hint, after)

    stacked = 1
    extra = []
    halves = chunk and halves_by_level(n, stages)
    before_last = max(len(stages) - 2, 0)
    for step, stage in enumerate(stages):
        if step == before_last:
            mask_poly, digits = digits_after(near(parts[0]))
        if halves and step == len(stages) - 1:
            matrix = (2 * 4 * 2 * cycle_blocks, 2 * DIGITS * DEPTH)
            mask_poly, change, digits, own_matrix = pl.pallas_call(
                functools.partial(early_kernel, n, chunk),
                out_shape=[pltpu.VMEM(mask_poly.shape, jnp.int32)] * 2
                + [pltpu.VMEM(digits.shape, jnp.bfloat16), pltpu.VMEM(matrix, jnp.bfloat16)],
                in_specs=[vmem] * 3,
                out_specs=[vmem] * 4,
                scratch_shapes=[pltpu.VMEM((n // 2 * chunk, LANES), jnp.int32)],
            )(near(mask_poly), near(digits), near(parts[0]))
            extra = [change, own_matrix]
        parts = [parts[0]] + [exchange(part, move) for part, move in zip(parts[1:], stage)]
        stacked *= len(parts)
        if step < len(stages) - 1:
            pieces = len(stages[step + 1]) + 1
            share = rows // pieces
            parts = pl.pallas_call(
                functools.partial(join_kernel, cycle_blocks, rows, chunk, len(parts)),
                out_shape=[pltpu.VMEM((share * (cycle_blocks + stacked * chunk), LANES), jnp.int32)] * pieces,
                in_specs=[anywhere] + [vmem] * len(parts),
                out_specs=[vmem] * pieces,
            )(near(mask_poly) if step == before_last else assignment, *map(near, parts))
            rows = share

    operands = [near(x) for x in (mask_poly, digits, *extra, *parts)]
    if not chunk:
        me = lax.axis_index("col")
        owners = assignment[jnp.stack(destinations(stages, me))] // polys
        keys = jnp.take(key_rows, owners, axis=0)[None]
        for stage in stages:
            cuts = jnp.split(keys, len(stage) + 1, axis=1)
            keys = jnp.concatenate([cuts[0]] + [exchange(x, move) for x, move in zip(cuts[1:], stage)], axis=0)
        places = jnp.zeros((n,), jnp.int32).at[jnp.stack(sources(stages, me))].set(jnp.arange(n, dtype=jnp.int32))
        operands.append(jnp.take(keys.reshape(n, key_width), places, axis=0).reshape(-1, LANES))
    return pl.pallas_call(
        functools.partial(late_kernel, n, chunk) if halves else functools.partial(pack_kernel, n, chunk, len(parts)),
        out_shape=jax.ShapeDtypeStruct((1, 2, cycle_width), jnp.float32),
        in_specs=[vmem] * len(operands),
        out_specs=vmem,
        scratch_shapes=[pltpu.VMEM((n * chunk, LANES), jnp.int32)] if chunk else [],
    )(*operands)


def solution(mesh):
    placed = (P("col", "grp"), P("grp", "col"), P("grp", "col"), P("grp", None), P("grp"))
    return jax.shard_map(
        on_device,
        mesh=mesh,
        in_specs=placed,
        out_specs=P(("grp", "col"), None, None),
        check_vma=False,
    )
```

```python
import functools

import jax
import jax.numpy as jnp
from jax import lax
from jax.experimental import pallas as pl
from jax.experimental.pallas import tpu as pltpu
from jax.sharding import PartitionSpec as P

LEVELS = 2
DIGITS = 2
LANES = 128
LOADS = 4
DEPTH = 64


def stages_of(n):
    bits = [1 << k for k in range(n.bit_length() - 1)]
    square = [(5, 1), (3, 1), (7, 0)] if len(bits) > 2 else [(b | 1, 0) for b in bits[1:2]]
    return [[(1, 0)]] + [square] * (len(square) > 0) + [[(b | 1, 0)] for b in bits[3:]]


def moved(move, i):
    mask, turn = move
    if turn:
        return i ^ mask ^ (((i >> 1 ^ i >> 2) & 1) * 6)
    return i ^ mask


def back(move):
    mask, turn = move
    return (mask ^ 6 if turn else mask, turn)


def follow(steps, i):
    for move in steps:
        i = moved(move, i)
    return i


def destinations(stages, me):
    rows = [[]]
    for stage in reversed(stages):
        rows = rows + [[move] + row for move in stage for row in rows]
    return [follow(row, me) for row in rows]


def sources(stages, me):
    blocks = [[]]
    for stage in stages:
        blocks = blocks + [[back(move)] + block for move in stage for block in blocks]
    return [follow(block, me) for block in blocks]


def answer_kernel(n, polys, assignment, *refs):
    database, (queries, key_rows), refs = refs[:LOADS], refs[LOADS : LOADS + 2], refs[LOADS + 2 :]
    outs, (rows, key_scratch) = refs[:-2], refs[-2:]
    clients = queries.shape[0]
    blocks = LOADS * database[0].shape[1] // LANES
    cycle_blocks = blocks // polys
    words = queries[...]
    bytes_ = [jnp.bitwise_and(jnp.right_shift(words, 8 * j), 255) for j in range(4)]
    lhs = jnp.concatenate(bytes_, axis=0).astype(jnp.float32).astype(jnp.bfloat16)
    rhs = jnp.concatenate([part[...] for part in database], axis=1).astype(jnp.float32).astype(jnp.bfloat16)
    sums = jnp.dot(lhs, rhs, preferred_element_type=jnp.float32).astype(jnp.int32)
    partial = sums[:clients]
    for j in range(1, 4):
        partial = partial + jnp.left_shift(sums[j * clients : (j + 1) * clients], 8 * j)
    for m in range(blocks):
        rows[pl.ds(m, clients, stride=blocks), :] = partial[:, m * LANES : (m + 1) * LANES]
    share = n // len(outs)
    chunk = outs[0].shape[0] // share - cycle_blocks
    for m in range(chunk):
        key_scratch[pl.ds(m, clients, stride=chunk), :] = key_rows[:, m * LANES : (m + 1) * LANES]
    me = lax.axis_index("col")
    for r, owner in enumerate(destinations(stages_of(n), me)):
        unit = assignment[owner]
        out, place = outs[r // share], r % share
        out[place * cycle_blocks : (place + 1) * cycle_blocks, :] = rows[
            pl.ds(pl.multiple_of(unit * cycle_blocks, cycle_blocks), cycle_blocks), :
        ]
        if chunk:
            first = share * cycle_blocks + place * chunk
            out[first : first + chunk, :] = key_scratch[pl.ds(unit // polys * chunk, chunk), :]


def join_kernel(cycle_blocks, rows, chunk, partners, after, *refs):
    del after
    parts, outs = refs[:partners], refs[partners:]
    share = rows // len(outs)
    cut = rows * cycle_blocks
    size = share * chunk
    for o, out in enumerate(outs):
        span = slice(o * share * cycle_blocks, (o + 1) * share * cycle_blocks)
        total = parts[0][span, :]
        for part in parts[1:]:
            total = total + part[span, :]
        out[: share * cycle_blocks, :] = total
        if chunk:
            stacked = (parts[0].shape[0] - cut) // (rows * chunk)
            for s in range(stacked * partners):
                source = cut + (s % stacked) * rows * chunk + o * size
                target = share * cycle_blocks + s * size
                out[target : target + size, :] = parts[s // stacked][source : source + size, :]


def shift_blocks(poly, count):
    blocks = poly.shape[0]
    whole, part = divmod(count % (2 * blocks), blocks)
    if part:
        row = lax.broadcasted_iota(jnp.int32, poly.shape, 0)
        poly = pltpu.roll(poly, part, 0)
        poly = jnp.where(row < part, -poly, poly)
    return -poly if whole else poly


def automorph(poly, level):
    blocks, lanes = poly.shape
    lane = lax.broadcasted_iota(jnp.int32, poly.shape, 1)
    period = 2 ** (level + 1)
    residue = jnp.bitwise_and(lane, period - 1)
    result = poly
    for m in range(1, period):
        result = jnp.where(residue == m, shift_blocks(poly, m * blocks // 2**level), result)
    return result


def toeplitz(word):
    blocks = word.shape[0]
    row = lax.broadcasted_iota(jnp.int32, (DEPTH, LANES), 0)
    lane = lax.broadcasted_iota(jnp.int32, (DEPTH, LANES), 1)
    inside = lane >= row
    turned = [
        pltpu.roll(jnp.broadcast_to(word[b : b + 1, :], (DEPTH, LANES)), 0, 1, stride=1, stride_axis=0)
        for b in range(blocks)
    ]
    columns = []
    for b in range(blocks):
        words = jnp.where(inside, turned[b], turned[b - 1])
        parts = []
        for j in range(4):
            part = jnp.bitwise_and(jnp.right_shift(words, 8 * j), 255).astype(jnp.float32)
            if b == 0:
                part = jnp.where(inside, part, -part)
            parts.append(part.astype(jnp.bfloat16))
        columns.append(jnp.concatenate(parts, axis=0))
    return jnp.concatenate(columns, axis=1)


def key_matrix(keys):
    lane = lax.broadcasted_iota(jnp.int32, keys[0][0].shape, 1)
    low = lane < DEPTH
    halves = [[None] * DIGITS for _ in range(4)]
    for p in range(2):
        for t in range(DIGITS):
            word = keys[t][p]
            other = pltpu.roll(word, DEPTH, 1)
            halves[2 * p][t] = jnp.where(low, word, jnp.left_shift(other, 8))
            halves[2 * p + 1][t] = jnp.where(low, other, jnp.left_shift(word, 8))
    rows = []
    for p in range(2):
        for s in range(4):
            for h in range(2):
                cut = [jnp.bitwise_and(jnp.right_shift(halves[2 * p + h][t], 8 * s), 255) for t in range(DIGITS)]
                rows.append(jnp.concatenate(cut, axis=1))
    return jnp.concatenate(rows, axis=0).astype(jnp.float32).astype(jnp.bfloat16)


def switch(matrix, digits, blocks):
    sums = jnp.dot(matrix, digits, preferred_element_type=jnp.float32).astype(jnp.int32)
    lane = lax.broadcasted_iota(jnp.int32, (blocks, LANES), 1)
    results = []
    for p in range(2):
        halves = []
        for h in range(2):
            total = None
            for m in range(blocks):
                joined = None
                for s in range(4):
                    first = ((p * 4 + s) * 2 + h) * blocks
                    piece = jnp.left_shift(sums[first : first + blocks, m * LANES : (m + 1) * LANES], 8 * s)
                    joined = piece if joined is None else joined + piece
                moved = shift_blocks(joined, m)
                total = moved if total is None else total + moved
            halves.append(total)
        turned = pltpu.roll(halves[1], DEPTH, 1)
        results.append(halves[0] + jnp.where(lane < DEPTH, shift_blocks(turned, 1), turned))
    return results


def digit_kernel(polys, assignment, hint, after, mask_out, digits_out):
    del after
    cycle_blocks = mask_out.shape[0]
    poly = assignment[lax.axis_index("col")] % polys
    row = hint[pl.ds(poly, 1), :]
    mask = jnp.concatenate([row[:, b * LANES : (b + 1) * LANES] for b in range(cycle_blocks)], axis=0)
    mask_out[...] = mask
    digits_out[...] = toeplitz(automorph(mask, 0))


def halves_by_level(n, stages):
    return LEVELS == 2 and stages[-1] == [(n // 2 + 1, 0)]


def level_matrix(keys, level, cycle_blocks):
    table = [
        [keys[pl.ds(((level * DIGITS + t) * 2 + p) * cycle_blocks, cycle_blocks), :] for p in range(2)]
        for t in range(DIGITS)
    ]
    return key_matrix(table)


def place_keys(total, chunk, cycle_blocks, origins, part, keys):
    for slot, origin in enumerate(origins):
        first = cycle_blocks + slot * chunk
        keys[pl.ds((origin & (total - 1)) * chunk, chunk), :] = part[first : first + chunk, :]


def early_kernel(n, chunk, mask_in, digits_in, part, mask_out, change_out, digits_out, matrix_out, keys):
    cycle_blocks = mask_in.shape[0]
    place_keys(n // 2, chunk, cycle_blocks, sources(stages_of(n)[:-1], lax.axis_index("col")), part, keys)
    matrix = level_matrix(keys, 0, cycle_blocks)
    matrix_out[...] = matrix
    early = lax.axis_index("col") < n // 2

    @pl.when(early)
    def _():
        change = switch(matrix, digits_in[...], cycle_blocks)
        mask = mask_in[...] + change[0]
        mask_out[...] = mask
        change_out[...] = change[1]
        digits_out[...] = toeplitz(automorph(mask, 1))

    @pl.when(jnp.logical_not(early))
    def _():
        mask_out[...] = mask_in[...]
        change_out[...] = jnp.zeros_like(change_out)
        digits_out[...] = digits_in[...]


def finish(level, mask, value, digits, matrices, packed):
    cycle_blocks = mask.shape[0]
    for i, matrix in enumerate(matrices):
        current = digits[...] if i == 0 else toeplitz(automorph(mask, level))
        change = switch(matrix(), current, cycle_blocks)
        mask = mask + change[0]
        value = value + automorph(value, level) + change[1]
        level += 1
    for p, words in enumerate((mask, value)):
        scaled = words.astype(jnp.float32) * 2.0**-32
        for b in range(cycle_blocks):
            packed[0, p : p + 1, b * LANES : (b + 1) * LANES] = scaled[b : b + 1, :]


def sum_answers(parts, cycle_blocks):
    value = parts[0][:cycle_blocks, :]
    for part in parts[1:]:
        value = value + part[:cycle_blocks, :]
    return value


def late_kernel(n, chunk, mask_in, digits, change_in, own_matrix, own, got, packed, keys):
    cycle_blocks = mask_in.shape[0]
    origins = sources(stages_of(n), lax.axis_index("col"))
    early = lax.axis_index("col") < n // 2

    def received():
        place_keys(n // 2, chunk, cycle_blocks, origins[n // 2 :], got, keys)
        return level_matrix(keys, 0, cycle_blocks)

    @pl.when(early)
    def _():
        value = sum_answers((own, got), cycle_blocks)
        finish(1, mask_in[...], value + automorph(value, 0) + change_in[...], digits, [received], packed)

    @pl.when(jnp.logical_not(early))
    def _():
        value = sum_answers((own, got), cycle_blocks)
        finish(0, mask_in[...], value, digits, [received, lambda: own_matrix[...]], packed)


def pack_kernel(n, chunk, partners, mask_in, digits, *refs):
    cycle_blocks = mask_in.shape[0]
    if chunk:
        *parts, packed, keys = refs
        stacked = n // partners
        away = sources(stages_of(n), lax.axis_index("col"))
        for i, part in enumerate(parts):
            place_keys(n, chunk, cycle_blocks, away[i * stacked : (i + 1) * stacked], part, keys)
    else:
        *parts, keys, packed = refs
    matrices = [functools.partial(level_matrix, keys, level, cycle_blocks) for level in range(LEVELS)]
    finish(0, mask_in[...], sum_answers(parts, cycle_blocks), digits, matrices, packed)


def near(x):
    return pltpu.with_memory_space_constraint(x, pltpu.VMEM)


def on_device(database, queries, key_rows, hint, assignment):
    n = lax.axis_size("col")
    polys, cycle_width = hint.shape
    clients = queries.shape[0]
    cycle_blocks = cycle_width // LANES
    key_width = key_rows.shape[1]
    stages = stages_of(n)
    vmem = pl.BlockSpec(memory_space=pltpu.VMEM)
    smem = pl.BlockSpec(memory_space=pltpu.SMEM)
    anywhere = pl.BlockSpec(memory_space=pl.ANY)
    chunk = key_width // LANES if key_width % LANES == 0 else 0

    def exchange(x, move):
        return lax.ppermute(x, "col", [(i, moved(move, i)) for i in range(n)])

    width = database.shape[1] // LOADS
    columns = [pl.BlockSpec((database.shape[0], width), lambda _, i=i: (0, i)) for i in range(LOADS)]
    pieces = len(stages[0]) + 1
    rows = n // pieces
    parts = pl.pallas_call(
        functools.partial(answer_kernel, n, polys),
        out_shape=[pltpu.VMEM((rows * (cycle_blocks + chunk), LANES), jnp.int32)] * pieces,
        grid=(1,),
        in_specs=[smem, *columns, vmem, vmem],
        out_specs=[vmem] * pieces,
        scratch_shapes=[
            pltpu.VMEM((clients * polys * cycle_blocks, LANES), jnp.int32),
            pltpu.VMEM((max(clients * chunk, 8), LANES), jnp.int32),
        ],
    )(assignment, *[database] * LOADS, queries, key_rows)
    def digits_after(after):
        return pl.pallas_call(
            functools.partial(digit_kernel, polys),
            out_shape=[
                pltpu.VMEM((cycle_blocks, LANES), jnp.int32),
                pltpu.VMEM((2 * DIGITS * DEPTH, cycle_width), jnp.bfloat16),
            ],
            in_specs=[smem, vmem, anywhere],
            out_specs=[vmem] * 2,
        )(assignment, hint, after)

    stacked = 1
    extra = []
    halves = chunk and halves_by_level(n, stages)
    before_last = max(len(stages) - 2, 0)
    for step, stage in enumerate(stages):
        if step == before_last:
            mask_poly, digits = digits_after(near(parts[0]))
        if halves and step == len(stages) - 1:
            matrix = (2 * 4 * 2 * cycle_blocks, 2 * DIGITS * DEPTH)
            mask_poly, change, digits, own_matrix = pl.pallas_call(
                functools.partial(early_kernel, n, chunk),
                out_shape=[pltpu.VMEM(mask_poly.shape, jnp.int32)] * 2
                + [pltpu.VMEM(digits.shape, jnp.bfloat16), pltpu.VMEM(matrix, jnp.bfloat16)],
                in_specs=[vmem] * 3,
                out_specs=[vmem] * 4,
                scratch_shapes=[pltpu.VMEM((n // 2 * chunk, LANES), jnp.int32)],
            )(near(mask_poly), near(digits), near(parts[0]))
            extra = [change, own_matrix]
        parts = [parts[0]] + [exchange(part, move) for part, move in zip(parts[1:], stage)]
        stacked *= len(parts)
        if step < len(stages) - 1:
            pieces = len(stages[step + 1]) + 1
            share = rows // pieces
            parts = pl.pallas_call(
                functools.partial(join_kernel, cycle_blocks, rows, chunk, len(parts)),
                out_shape=[pltpu.VMEM((share * (cycle_blocks + stacked * chunk), LANES), jnp.int32)] * pieces,
                in_specs=[anywhere] + [vmem] * len(parts),
                out_specs=[vmem] * pieces,
            )(near(mask_poly) if step == before_last else assignment, *map(near, parts))
            rows = share

    operands = [near(x) for x in (mask_poly, digits, *extra, *parts)]
    if not chunk:
        me = lax.axis_index("col")
        owners = assignment[jnp.stack(destinations(stages, me))] // polys
        keys = jnp.take(key_rows, owners, axis=0)[None]
        for stage in stages:
            cuts = jnp.split(keys, len(stage) + 1, axis=1)
            keys = jnp.concatenate([cuts[0]] + [exchange(x, move) for x, move in zip(cuts[1:], stage)], axis=0)
        places = jnp.zeros((n,), jnp.int32).at[jnp.stack(sources(stages, me))].set(jnp.arange(n, dtype=jnp.int32))
        operands.append(jnp.take(keys.reshape(n, key_width), places, axis=0).reshape(-1, LANES))
    return pl.pallas_call(
        functools.partial(late_kernel, n, chunk) if halves else functools.partial(pack_kernel, n, chunk, len(parts)),
        out_shape=jax.ShapeDtypeStruct((1, 2, cycle_width), jnp.float32),
        in_specs=[vmem] * len(operands),
        out_specs=vmem,
        scratch_shapes=[pltpu.VMEM((n * chunk, LANES), jnp.int32)] if chunk else [],
    )(*operands)


def solution(mesh):
    placed = (P("col", "grp"), P("grp", "col"), P("grp", "col"), P("grp", None), P("grp"))
    return jax.shard_map(
        on_device,
        mesh=mesh,
        in_specs=placed,
        out_specs=P(("grp", "col"), None, None),
        check_vma=False,
    )
```

```python
import functools

import jax
import jax.numpy as jnp
from jax import lax
from jax.experimental import pallas as pl
from jax.experimental.pallas import tpu as pltpu
from jax.sharding import PartitionSpec as P

LEVELS = 2
DIGITS = 2
LANES = 128
LOADS = 4
DEPTH = 64


def stages_of(n):
    bits = [1 << k for k in range(n.bit_length() - 1)]
    square = [(5, 1), (3, 1), (7, 0)] if len(bits) > 2 else [(b | 1, 0) for b in bits[1:2]]
    return [[(1, 0)]] + [square] * (len(square) > 0) + [[(b | 1, 0)] for b in bits[3:]]


def moved(move, i):
    mask, turn = move
    if turn:
        return i ^ mask ^ (((i >> 1 ^ i >> 2) & 1) * 6)
    return i ^ mask


def back(move):
    mask, turn = move
    return (mask ^ 6 if turn else mask, turn)


def follow(steps, i):
    for move in steps:
        i = moved(move, i)
    return i


def destinations(stages, me):
    rows = [[]]
    for stage in reversed(stages):
        rows = rows + [[move] + row for move in stage for row in rows]
    return [follow(row, me) for row in rows]


def sources(stages, me):
    blocks = [[]]
    for stage in stages:
        blocks = blocks + [[back(move)] + block for move in stage for block in blocks]
    return [follow(block, me) for block in blocks]


def answer_kernel(n, polys, assignment, *refs):
    database, (queries, key_rows), refs = refs[:LOADS], refs[LOADS : LOADS + 2], refs[LOADS + 2 :]
    outs, (rows, key_scratch) = refs[:-2], refs[-2:]
    clients = queries.shape[0]
    blocks = LOADS * database[0].shape[1] // LANES
    cycle_blocks = blocks // polys
    words = queries[...]
    bytes_ = [jnp.bitwise_and(jnp.right_shift(words, 8 * j), 255) for j in range(4)]
    lhs = jnp.concatenate(bytes_, axis=0).astype(jnp.float32).astype(jnp.bfloat16)
    rhs = jnp.concatenate([part[...].astype(jnp.float32).astype(jnp.bfloat16) for part in database], axis=1)
    sums = jnp.dot(lhs, rhs, preferred_element_type=jnp.float32).astype(jnp.int32)
    partial = sums[:clients]
    for j in range(1, 4):
        partial = partial + jnp.left_shift(sums[j * clients : (j + 1) * clients], 8 * j)
    for m in range(blocks):
        rows[pl.ds(m, clients, stride=blocks), :] = partial[:, m * LANES : (m + 1) * LANES]
    share = n // len(outs)
    chunk = outs[0].shape[0] // share - cycle_blocks
    for m in range(chunk):
        key_scratch[pl.ds(m, clients, stride=chunk), :] = key_rows[:, m * LANES : (m + 1) * LANES]
    me = lax.axis_index("col")
    for r, owner in enumerate(destinations(stages_of(n), me)):
        unit = assignment[owner]
        out, place = outs[r // share], r % share
        out[place * cycle_blocks : (place + 1) * cycle_blocks, :] = rows[
            pl.ds(pl.multiple_of(unit * cycle_blocks, cycle_blocks), cycle_blocks), :
        ]
        if chunk:
            first = share * cycle_blocks + place * chunk
            out[first : first + chunk, :] = key_scratch[pl.ds(unit // polys * chunk, chunk), :]


def join_kernel(cycle_blocks, rows, chunk, partners, after, *refs):
    del after
    parts, outs = refs[:partners], refs[partners:]
    share = rows // len(outs)
    cut = rows * cycle_blocks
    size = share * chunk
    for o, out in enumerate(outs):
        span = slice(o * share * cycle_blocks, (o + 1) * share * cycle_blocks)
        total = parts[0][span, :]
        for part in parts[1:]:
            total = total + part[span, :]
        out[: share * cycle_blocks, :] = total
        if chunk:
            stacked = (parts[0].shape[0] - cut) // (rows * chunk)
            for s in range(stacked * partners):
                source = cut + (s % stacked) * rows * chunk + o * size
                target = share * cycle_blocks + s * size
                out[target : target + size, :] = parts[s // stacked][source : source + size, :]


def shift_blocks(poly, count):
    blocks = poly.shape[0]
    whole, part = divmod(count % (2 * blocks), blocks)
    if part:
        row = lax.broadcasted_iota(jnp.int32, poly.shape, 0)
        poly = pltpu.roll(poly, part, 0)
        poly = jnp.where(row < part, -poly, poly)
    return -poly if whole else poly


def automorph(poly, level):
    blocks, lanes = poly.shape
    lane = lax.broadcasted_iota(jnp.int32, poly.shape, 1)
    period = 2 ** (level + 1)
    residue = jnp.bitwise_and(lane, period - 1)
    result = poly
    for m in range(1, period):
        result = jnp.where(residue == m, shift_blocks(poly, m * blocks // 2**level), result)
    return result


def toeplitz(word):
    blocks = word.shape[0]
    row = lax.broadcasted_iota(jnp.int32, (DEPTH, LANES), 0)
    lane = lax.broadcasted_iota(jnp.int32, (DEPTH, LANES), 1)
    inside = lane >= row
    turned = [
        pltpu.roll(jnp.broadcast_to(word[b : b + 1, :], (DEPTH, LANES)), 0, 1, stride=1, stride_axis=0)
        for b in range(blocks)
    ]
    columns = []
    for b in range(blocks):
        words = jnp.where(inside, turned[b], turned[b - 1])
        parts = []
        for j in range(4):
            part = jnp.bitwise_and(jnp.right_shift(words, 8 * j), 255).astype(jnp.float32)
            if b == 0:
                part = jnp.where(inside, part, -part)
            parts.append(part.astype(jnp.bfloat16))
        columns.append(jnp.concatenate(parts, axis=0))
    return jnp.concatenate(columns, axis=1)


def key_matrix(keys):
    lane = lax.broadcasted_iota(jnp.int32, keys[0][0].shape, 1)
    low = lane < DEPTH
    halves = [[None] * DIGITS for _ in range(4)]
    for p in range(2):
        for t in range(DIGITS):
            word = keys[t][p]
            other = pltpu.roll(word, DEPTH, 1)
            halves[2 * p][t] = jnp.where(low, word, jnp.left_shift(other, 8))
            halves[2 * p + 1][t] = jnp.where(low, other, jnp.left_shift(word, 8))
    rows = []
    for p in range(2):
        for s in range(4):
            for h in range(2):
                cut = [jnp.bitwise_and(jnp.right_shift(halves[2 * p + h][t], 8 * s), 255) for t in range(DIGITS)]
                rows.append(jnp.concatenate(cut, axis=1))
    return jnp.concatenate(rows, axis=0).astype(jnp.float32).astype(jnp.bfloat16)


def switch(matrix, digits, blocks):
    sums = jnp.dot(matrix, digits, preferred_element_type=jnp.float32).astype(jnp.int32)
    lane = lax.broadcasted_iota(jnp.int32, (blocks, LANES), 1)
    results = []
    for p in range(2):
        halves = []
        for h in range(2):
            total = None
            for m in range(blocks):
                joined = None
                for s in range(4):
                    first = ((p * 4 + s) * 2 + h) * blocks
                    piece = jnp.left_shift(sums[first : first + blocks, m * LANES : (m + 1) * LANES], 8 * s)
                    joined = piece if joined is None else joined + piece
                moved = shift_blocks(joined, m)
                total = moved if total is None else total + moved
            halves.append(total)
        turned = pltpu.roll(halves[1], DEPTH, 1)
        results.append(halves[0] + jnp.where(lane < DEPTH, shift_blocks(turned, 1), turned))
    return results


def digit_kernel(polys, assignment, hint, after, mask_out, digits_out):
    del after
    cycle_blocks = mask_out.shape[0]
    poly = assignment[lax.axis_index("col")] % polys
    row = hint[pl.ds(poly, 1), :]
    mask = jnp.concatenate([row[:, b * LANES : (b + 1) * LANES] for b in range(cycle_blocks)], axis=0)
    mask_out[...] = mask
    digits_out[...] = toeplitz(automorph(mask, 0))


def halves_by_level(n, stages):
    return LEVELS == 2 and stages[-1] == [(n // 2 + 1, 0)]


def level_matrix(keys, level, cycle_blocks):
    table = [
        [keys[pl.ds(((level * DIGITS + t) * 2 + p) * cycle_blocks, cycle_blocks), :] for p in range(2)]
        for t in range(DIGITS)
    ]
    return key_matrix(table)


def place_keys(total, chunk, cycle_blocks, origins, part, keys):
    for slot, origin in enumerate(origins):
        first = cycle_blocks + slot * chunk
        keys[pl.ds((origin & (total - 1)) * chunk, chunk), :] = part[first : first + chunk, :]


def early_kernel(n, chunk, mask_in, digits_in, part, mask_out, change_out, digits_out, matrix_out, keys):
    cycle_blocks = mask_in.shape[0]
    place_keys(n // 2, chunk, cycle_blocks, sources(stages_of(n)[:-1], lax.axis_index("col")), part, keys)
    matrix = level_matrix(keys, 0, cycle_blocks)
    matrix_out[...] = matrix
    early = lax.axis_index("col") < n // 2

    @pl.when(early)
    def _():
        change = switch(matrix, digits_in[...], cycle_blocks)
        mask = mask_in[...] + change[0]
        mask_out[...] = mask
        change_out[...] = change[1]
        digits_out[...] = toeplitz(automorph(mask, 1))

    @pl.when(jnp.logical_not(early))
    def _():
        mask_out[...] = mask_in[...]
        change_out[...] = jnp.zeros_like(change_out)
        digits_out[...] = digits_in[...]


def finish(level, mask, value, digits, matrices, packed):
    cycle_blocks = mask.shape[0]
    for i, matrix in enumerate(matrices):
        current = digits[...] if i == 0 else toeplitz(automorph(mask, level))
        change = switch(matrix(), current, cycle_blocks)
        mask = mask + change[0]
        value = value + automorph(value, level) + change[1]
        level += 1
    scaled = [words.astype(jnp.float32) * 2.0**-32 for words in (mask, value)]
    for b in range(cycle_blocks):
        packed[0, :, b * LANES : (b + 1) * LANES] = jnp.concatenate([words[b : b + 1, :] for words in scaled], axis=0)


def sum_answers(parts, cycle_blocks):
    value = parts[0][:cycle_blocks, :]
    for part in parts[1:]:
        value = value + part[:cycle_blocks, :]
    return value


def late_kernel(n, chunk, mask_in, digits, change_in, own_matrix, own, got, packed, keys):
    cycle_blocks = mask_in.shape[0]
    origins = sources(stages_of(n), lax.axis_index("col"))
    early = lax.axis_index("col") < n // 2

    def received():
        place_keys(n // 2, chunk, cycle_blocks, origins[n // 2 :], got, keys)
        return level_matrix(keys, 0, cycle_blocks)

    @pl.when(early)
    def _():
        value = sum_answers((own, got), cycle_blocks)
        finish(1, mask_in[...], value + automorph(value, 0) + change_in[...], digits, [received], packed)

    @pl.when(jnp.logical_not(early))
    def _():
        value = sum_answers((own, got), cycle_blocks)
        finish(0, mask_in[...], value, digits, [received, lambda: own_matrix[...]], packed)


def pack_kernel(n, chunk, partners, mask_in, digits, *refs):
    cycle_blocks = mask_in.shape[0]
    if chunk:
        *parts, packed, keys = refs
        stacked = n // partners
        away = sources(stages_of(n), lax.axis_index("col"))
        for i, part in enumerate(parts):
            place_keys(n, chunk, cycle_blocks, away[i * stacked : (i + 1) * stacked], part, keys)
    else:
        *parts, keys, packed = refs
    matrices = [functools.partial(level_matrix, keys, level, cycle_blocks) for level in range(LEVELS)]
    finish(0, mask_in[...], sum_answers(parts, cycle_blocks), digits, matrices, packed)


def near(x):
    return pltpu.with_memory_space_constraint(x, pltpu.VMEM)


def on_device(database, queries, key_rows, hint, assignment):
    n = lax.axis_size("col")
    polys, cycle_width = hint.shape
    clients = queries.shape[0]
    cycle_blocks = cycle_width // LANES
    key_width = key_rows.shape[1]
    stages = stages_of(n)
    vmem = pl.BlockSpec(memory_space=pltpu.VMEM)
    smem = pl.BlockSpec(memory_space=pltpu.SMEM)
    anywhere = pl.BlockSpec(memory_space=pl.ANY)
    chunk = key_width // LANES if key_width % LANES == 0 else 0

    def exchange(x, move):
        return lax.ppermute(x, "col", [(i, moved(move, i)) for i in range(n)])

    width = database.shape[1] // LOADS
    columns = [pl.BlockSpec((database.shape[0], width), lambda _, i=i: (0, i)) for i in range(LOADS)]
    pieces = len(stages[0]) + 1
    rows = n // pieces
    parts = pl.pallas_call(
        functools.partial(answer_kernel, n, polys),
        out_shape=[pltpu.VMEM((rows * (cycle_blocks + chunk), LANES), jnp.int32)] * pieces,
        grid=(1,),
        in_specs=[smem, *columns, vmem, vmem],
        out_specs=[vmem] * pieces,
        scratch_shapes=[
            pltpu.VMEM((clients * polys * cycle_blocks, LANES), jnp.int32),
            pltpu.VMEM((max(clients * chunk, 8), LANES), jnp.int32),
        ],
    )(assignment, *[database] * LOADS, queries, key_rows)
    def digits_after(after):
        return pl.pallas_call(
            functools.partial(digit_kernel, polys),
            out_shape=[
                pltpu.VMEM((cycle_blocks, LANES), jnp.int32),
                pltpu.VMEM((2 * DIGITS * DEPTH, cycle_width), jnp.bfloat16),
            ],
            in_specs=[smem, vmem, anywhere],
            out_specs=[vmem] * 2,
        )(assignment, hint, after)

    stacked = 1
    extra = []
    halves = chunk and halves_by_level(n, stages)
    before_last = max(len(stages) - 2, 0)
    for step, stage in enumerate(stages):
        if step == before_last:
            mask_poly, digits = digits_after(near(parts[0]))
        if halves and step == len(stages) - 1:
            matrix = (2 * 4 * 2 * cycle_blocks, 2 * DIGITS * DEPTH)
            mask_poly, change, digits, own_matrix = pl.pallas_call(
                functools.partial(early_kernel, n, chunk),
                out_shape=[pltpu.VMEM(mask_poly.shape, jnp.int32)] * 2
                + [pltpu.VMEM(digits.shape, jnp.bfloat16), pltpu.VMEM(matrix, jnp.bfloat16)],
                in_specs=[vmem] * 3,
                out_specs=[vmem] * 4,
                scratch_shapes=[pltpu.VMEM((n // 2 * chunk, LANES), jnp.int32)],
            )(near(mask_poly), near(digits), near(parts[0]))
            extra = [change, own_matrix]
        parts = [parts[0]] + [exchange(part, move) for part, move in zip(parts[1:], stage)]
        stacked *= len(parts)
        if step < len(stages) - 1:
            pieces = len(stages[step + 1]) + 1
            share = rows // pieces
            parts = pl.pallas_call(
                functools.partial(join_kernel, cycle_blocks, rows, chunk, len(parts)),
                out_shape=[pltpu.VMEM((share * (cycle_blocks + stacked * chunk), LANES), jnp.int32)] * pieces,
                in_specs=[anywhere] + [vmem] * len(parts),
                out_specs=[vmem] * pieces,
            )(near(mask_poly) if step == before_last else assignment, *map(near, parts))
            rows = share

    operands = [near(x) for x in (mask_poly, digits, *extra, *parts)]
    if not chunk:
        me = lax.axis_index("col")
        owners = assignment[jnp.stack(destinations(stages, me))] // polys
        keys = jnp.take(key_rows, owners, axis=0)[None]
        for stage in stages:
            cuts = jnp.split(keys, len(stage) + 1, axis=1)
            keys = jnp.concatenate([cuts[0]] + [exchange(x, move) for x, move in zip(cuts[1:], stage)], axis=0)
        places = jnp.zeros((n,), jnp.int32).at[jnp.stack(sources(stages, me))].set(jnp.arange(n, dtype=jnp.int32))
        operands.append(jnp.take(keys.reshape(n, key_width), places, axis=0).reshape(-1, LANES))
    return pl.pallas_call(
        functools.partial(late_kernel, n, chunk) if halves else functools.partial(pack_kernel, n, chunk, len(parts)),
        out_shape=jax.ShapeDtypeStruct((1, 2, cycle_width), jnp.float32),
        in_specs=[vmem] * len(operands),
        out_specs=vmem,
        scratch_shapes=[pltpu.VMEM((n * chunk, LANES), jnp.int32)] if chunk else [],
    )(*operands)


def solution(mesh):
    placed = (P("col", "grp"), P("grp", "col"), P("grp", "col"), P("grp", None), P("grp"))
    return jax.shard_map(
        on_device,
        mesh=mesh,
        in_specs=placed,
        out_specs=P(("grp", "col"), None, None),
        check_vma=False,
    )
```
